32 devices in a mesh: dp: 8 (over z, y), mp: 4 (over x, core).
Axes of the slice: x: 2, y: 2, z: 4, core: 2. Of those that a mesh axis runs over, the one named last changes fastest.
Arguments:
- table: float32 [32768, 1024], P('dp', 'mp'), may hold values from -6 to 6
- q_weight: float32 [1024, 1024], P(None, 'mp'), may hold values from -0.1875 to 0.1875
- q_bias: float32 [1024], P('mp'), may hold values from -3 to 3
- w_weight: float32 [2048, 1024], P(None, 'mp'), may hold values from -0.125 to 0.125
- w_bias: float32 [1024], P('mp'), may hold values from -3 to 3
- neighbours: int32 [2048, 50], P('dp'), may hold values from 0 to 32767, as said below
- counts: int32 [2048], P('dp'), may hold values from 5 to 50
- importance: float32 [2048, 50], P('dp'), may hold values from 0.05 to 1
- cotangent: float32 [2048, 1024], P('dp', 'mp'), may hold values from -6 to 6
Outputs:
- embedding: float32 [2048, 1024], P('dp', 'mp')
- table_grad: float32 [32768, 1024], P('dp', 'mp')
- q_weight_grad: float32 [1024, 1024], P(None, 'mp')
- q_bias_grad: float32 [1024], P('mp')
- w_weight_grad: float32 [2048, 1024], P(None, 'mp')
- w_bias_grad: float32 [1024], P('mp')
- penalty: float32 [], replicated
The draws below stay inside these ranges and needn't reach their ends.
Inputs may be any that keep to these rules, and one draw needn't show every extreme that they name: `neighbours`: table row r belongs to index r // 4096 of dp. Among the 12800 ids of one index's nodes (padded slots included) at most 2400 belong to any one index of dp, and this many is reached by some index of dp for every node block.
All inputs are finite; a program needn't handle non-finite values.
Results may differ from the reference program's by a relative error of at most 0.0074.
Values may be sent and summed in bfloat16 or wider, within the bound.
No kernel may reach another device: no remote copies, remote signals or barrier semaphores. Data moves between devices by JAX's collectives and lax.ppermute only.
A program may use at most 256 MiB of HBM per device.

```python
import math
import jax
import jax.numpy as jnp
from jax import lax

D = 1024
K = 50
NODE_DEV = 256
ROW_DEV = 4096
NODES = 2048
ROWS = 32768
N_DP = 8


def draw_neighbours(key, part):
    key = jax.random.fold_in(key, 7)
    slot_count = NODE_DEV * K
    share_each = slot_count // N_DP
    position = jnp.arange(slot_count, dtype=jnp.int32)
    group_index = position // (4 * share_each)
    within = position % (4 * share_each)
    role_index = (within >= 3 * share_each // 2).astype(jnp.int32) + (within >= 5 * share_each // 2).astype(jnp.int32) + (within >= 7 * share_each // 2).astype(jnp.int32)

    def one_device(device_key):
        split_keys = jax.random.split(device_key, 3)
        owners = jax.random.permutation(split_keys[0], N_DP).astype(jnp.int32)
        slot_owner = owners[4 * group_index + role_index]
        shuffled = jax.random.permutation(split_keys[1], slot_owner)
        local_rows = jax.random.randint(split_keys[2], (slot_count,), 0, ROW_DEV, dtype=jnp.int32)
        return (shuffled * ROW_DEV + local_rows).astype(jnp.int32)
    device_keys = jax.random.split(key, N_DP)
    return jax.vmap(one_device)(device_keys).reshape(NODES, K)


def touch_ends(values, own_key, low, largest):
    longest = values.shape.index(max(values.shape))
    spots = []
    for shift in (0, 1):
        where = [jax.random.randint(jax.random.fold_in(own_key, axis), (), 0, length) for axis, length in enumerate(values.shape)]
        where[longest] = (where[longest] + shift) % values.shape[longest]
        spots.append(tuple(where))
    return values.at[spots[0]].set(low).at[spots[1]].set(largest)


def level_of(stream_key, extent, shards, low, top_value):
    gain = 1.0
    for axis_at, parts in shards:
        draws = jax.random.uniform(jax.random.fold_in(jax.random.fold_in(stream_key, 6), axis_at), (parts,), jnp.float32, low / len(shards), top_value / len(shards))
        gain = gain * jnp.repeat(jnp.exp(draws), extent[axis_at] // parts).reshape((-1,) + (1,) * (len(extent) - 1 - axis_at))
    return gain


def noise(stream_key, dims, spread, reach, shards=(), kind=jnp.bfloat16):
    factor_of = level_of(stream_key, dims, shards, -0.22, 0.18) if shards else 1.0
    result = jax.random.normal(stream_key, dims, jnp.float32) * spread * factor_of
    return jnp.minimum(jnp.maximum(result, -reach), reach).astype(kind)


def setup_inputs(seed: int = 0) -> dict:
    arg_keys = jax.random.split(jax.random.key(seed), 10)
    table = noise(arg_keys[0], (ROWS, D), 1.0, 6.0, ((0, 8), (1, 4)), jnp.float32)
    q_weight = noise(arg_keys[1], (D, D), D ** -0.5, 0.1875, ((1, 4),), jnp.float32)
    q_bias = noise(arg_keys[2], (D,), 0.5, 3.0, ((0, 4),), jnp.float32)
    w_weight = noise(arg_keys[3], (2 * D, D), (2 * D) ** -0.5, 0.125, ((1, 4),), jnp.float32)
    w_bias = noise(arg_keys[4], (D,), 0.5, 3.0, ((0, 4),), jnp.float32)
    neighbours = draw_neighbours(jax.random.fold_in(arg_keys[9], 71), 0)
    counts = touch_ends(jax.random.randint(arg_keys[6], (NODES,), 5, K + 1), jax.random.fold_in(arg_keys[6], 1), 5, K).astype(jnp.int32)
    importance = jnp.clip(jnp.exp(math.log(1.0) - 2.9957323 * jax.random.uniform(arg_keys[7], (NODES, K), jnp.float32) ** level_of(arg_keys[7], (NODES, K), ((0, 8),), -0.2, 0.2)), 0.05, 1.0)
    cotangent = noise(arg_keys[8], (NODES, D), 1.0, 6.0, ((0, 8), (1, 4)), jnp.float32)
    return dict(table=table, q_weight=q_weight, q_bias=q_bias, w_weight=w_weight, w_bias=w_bias, neighbours=neighbours, counts=counts, importance=importance, cotangent=cotangent)


epsilon = 1e-06
penalty_rate = 0.01
highest = lax.Precision.HIGHEST

@jax.custom_vjp
def low(v):
    return lax.optimization_barrier(v.astype(jnp.bfloat16)).astype(jnp.float32)

@jax.custom_vjp
def low_back(v):
    return v

def low_keep(v):
    return (low(v), None)

def low_pass(kept, grad):
    return (grad,)

def back_keep(v):
    return (v, None)

def back_low(kept, grad):
    return (low(grad),)
low.defvjp(low_keep, low_pass)
low_back.defvjp(back_keep, back_low)

def layer(table, q_weight, q_bias, w_weight, w_bias, neighbours, weights):
    table_low = low(table)
    q_low = low(q_weight)
    w_low = low(w_weight)
    block_nodes = 256 if NODES % 256 == 0 else NODE_DEV

    def block(pieces):
        block_ids, block_weights = pieces
        gathered = table_low[block_ids.reshape(-1)]
        hidden_pre = low_back(jnp.dot(gathered, q_low, precision=highest) + q_bias)
        hidden = jax.nn.gelu(hidden_pre).reshape(block_nodes, K, D)
        return jnp.einsum('nk,nkd->nd', block_weights, hidden, precision=highest)
    pooled = lax.map(jax.checkpoint(block), (neighbours.reshape(-1, block_nodes, K), weights.reshape(-1, block_nodes, K)))
    pooled = low(pooled.reshape(NODES, D))
    node_index = jnp.arange(NODES, dtype=jnp.int32)
    self_ids = (node_index // NODE_DEV * ROW_DEV + node_index % NODE_DEV).astype(jnp.int32)
    joined = jnp.concatenate([table_low[self_ids], pooled], axis=1)
    output_pre = low_back(jnp.dot(joined, w_low, precision=highest) + w_bias)
    activated = jax.nn.gelu(output_pre)
    squares = lax.optimization_barrier(jnp.sum(activated * activated, axis=1))
    embedding = activated * lax.rsqrt(squares + epsilon)[:, None]
    penalty = penalty_rate * jnp.sum(squares) / NODES
    return (embedding, penalty)

def reference(table, q_weight, q_bias, w_weight, w_bias, neighbours, counts, importance, cotangent):
    present = (jnp.arange(K, dtype=jnp.int32)[None, :] < counts[:, None]).astype(importance.dtype)
    raw_weights = importance * present
    weights = raw_weights / lax.optimization_barrier(jnp.sum(raw_weights, axis=1, keepdims=True))

    def forward(table_in, q_in, qb_in, w_in, wb_in):
        return layer(table_in, q_in, qb_in, w_in, wb_in, neighbours, weights)
    (embedding, penalty), pullback = jax.vjp(forward, table, q_weight, q_bias, w_weight, w_bias)
    grads = pullback((cotangent, jnp.ones_like(penalty)))
    return (embedding, grads[0], grads[1], grads[2], grads[3], grads[4], penalty)
```

```python
import functools

import jax
import jax.numpy as jnp
from jax import lax
from jax.experimental import pallas as pl
from jax.experimental.pallas import tpu as pltpu
from jax.sharding import PartitionSpec as P

epsilon = 1e-06
penalty_rate = 0.01
bf16, f32 = jnp.bfloat16, jnp.float32
bucket_rows = 256
lane_tile = 128


def dot(a, b, contract):
    return lax.dot_general(a, b, ((contract[:1], contract[1:]), ((), ())), preferred_element_type=f32)


def gelu_parts(values):
    c = 0.7978845608028654
    squared = values * values
    t = jnp.tanh(c * values * (1.0 + 0.044715 * squared))
    half = 0.5 * (1.0 + t)
    slope = half + 0.5 * values * (1.0 - t * t) * (c * (1.0 + 3 * 0.044715 * squared))
    return values * half, slope


def params(**kwargs):
    return pltpu.CompilerParams(vmem_limit_bytes=56 * 1024 * 1024, **kwargs)


def spread_kernel(row_dev, base_ref, slots_ref, out_ref):
    slots_node = slots_ref.shape[2]
    weight = slots_ref[0, 1]
    local = (slots_ref[0, 0] - base_ref[0].astype(f32)).astype(jnp.int32)
    owned = (local >= 0) & (local < row_dev) & (weight != 0.0)
    bucket = jnp.where(owned, local // bucket_rows, -1)
    within = (local - bucket * bucket_rows).astype(f32)
    index = lax.broadcasted_iota(jnp.int32, bucket.shape, 0)
    rank = jnp.zeros(bucket.shape, jnp.int32)
    for k in range(slots_node - 1):
        same = (bucket == bucket[k : k + 1, :]) & (index > k)
        rank = rank + jnp.where(same, 1, 0)
    code = jnp.where(owned, bucket * 64 + rank, -1)
    depth = jnp.max(jnp.where(owned, rank + 1, 0).astype(f32)).astype(jnp.int32)
    row_index = lax.broadcasted_iota(jnp.int32, (bucket_rows, lane_tile), 0).astype(f32)

    def one_bucket(b, carry):
        def body(j, total):
            hit = code == b * 64 + j
            row = jnp.sum(jnp.where(hit, within, 0.0), axis=0, keepdims=True)
            amount = jnp.sum(jnp.where(hit, weight, 0.0), axis=0, keepdims=True)
            return total + jnp.where(row_index == row, amount, 0.0)

        total = lax.fori_loop(0, depth, body, jnp.zeros((bucket_rows, lane_tile), f32))
        out_ref[pl.ds(pl.multiple_of(b * bucket_rows, bucket_rows), bucket_rows), :] = total.astype(bf16)
        return carry

    lax.fori_loop(0, row_dev // bucket_rows, one_bucket, 0)


def spread(base, slots, row_dev):
    groups, _, slots_node, node_dev = slots.shape
    tiles = node_dev // lane_tile
    return pl.pallas_call(
        functools.partial(spread_kernel, row_dev),
        grid=(groups, tiles),
        in_specs=[
            pl.BlockSpec(memory_space=pltpu.SMEM),
            pl.BlockSpec((1, 2, slots_node, lane_tile), lambda i, t: (i, 0, 0, t)),
        ],
        out_specs=pl.BlockSpec((row_dev, lane_tile), lambda i, t: (0, i * tiles + t)),
        out_shape=jax.ShapeDtypeStruct((row_dev, groups * node_dev), bf16),
        compiler_params=params(),
        name="spread",
    )(base, slots)


def pool_kernel(table_ref, q_ref, bias_ref, spread_ref, slope_ref, pooled_ref, total_ref):
    step = pl.program_id(0)
    width = table_ref.shape[2]
    pre = bias_ref[...]
    for m in range(table_ref.shape[0]):
        pre = pre + dot(table_ref[m], q_ref[m * width : (m + 1) * width, :], (1, 0))
    hidden, slope = gelu_parts(pre)
    slope_ref[...] = slope.astype(bf16)
    part = dot(hidden.astype(bf16), spread_ref[...], (0, 0))

    @pl.when(step == 0)
    def _():
        total_ref[...] = part

    @pl.when(step > 0)
    def _():
        total_ref[...] += part

    @pl.when(step == pl.num_programs(0) - 1)
    def _():
        groups, _, node_dev = pooled_ref.shape
        for g in range(groups):
            pooled_ref[g] = total_ref[:, g * node_dev : (g + 1) * node_dev].astype(bf16)


def pool(table4, q_low, bias, matrix, node_dev):
    sides, row_dev, width = table4.shape
    nodes = matrix.shape[1]
    columns = q_low.shape[1]
    block = min(row_dev, 512 * 2048 // nodes)
    groups = nodes // node_dev
    return pl.pallas_call(
        pool_kernel,
        grid=(row_dev // block,),
        in_specs=[
            pl.BlockSpec((sides, block, width), lambda i: (0, i, 0)),
            pl.BlockSpec(q_low.shape, lambda i: (0, 0)),
            pl.BlockSpec((1, columns), lambda i: (0, 0)),
            pl.BlockSpec((block, nodes), lambda i: (i, 0)),
        ],
        out_specs=(
            pl.BlockSpec((block, columns), lambda i: (i, 0)),
            pl.BlockSpec((groups, columns, node_dev), lambda i: (0, 0, 0)),
        ),
        out_shape=(
            jax.ShapeDtypeStruct((row_dev, columns), bf16),
            jax.ShapeDtypeStruct((groups, columns, node_dev), bf16),
        ),
        scratch_shapes=[pltpu.VMEM((columns, nodes), f32)],
        compiler_params=params(),
        name="pool",
    )(table4, q_low, bias.reshape(1, columns), matrix)


def combine_kernel(self_ref, pooled_ref, w_ref, bias_ref, cotangent_ref, pre_ref, sums_ref):
    sides, nodes, width = self_ref.shape
    pre = bias_ref[...]
    for m in range(sides):
        pre = pre + dot(self_ref[m], w_ref[m * width : (m + 1) * width, :], (1, 0))
    for m in range(sides):
        at = (sides + m) * width
        pre = pre + dot(pooled_ref[m], w_ref[at : at + width, :], (0, 0))
    pre_ref[...] = pre
    activated, _ = gelu_parts(pre)
    sums_ref[:, 0:1] = jnp.sum(activated * activated, axis=1, keepdims=True)
    sums_ref[:, 1:2] = jnp.sum(activated * cotangent_ref[...], axis=1, keepdims=True)


def combine(self4, pooled4, w_low, bias, cotangent):
    nodes, columns = cotangent.shape
    return pl.pallas_call(
        combine_kernel,
        out_shape=(
            jax.ShapeDtypeStruct((nodes, columns), f32),
            jax.ShapeDtypeStruct((nodes, 2), f32),
        ),
        compiler_params=params(),
        name="combine",
    )(self4, pooled4, w_low, bias.reshape(1, columns), cotangent)


def combine_back_kernel(
    node_total, pre_ref, sums_ref, cotangent_ref, self_ref, pooled_ref, w_ref, emb_ref, w_grad_ref, wb_grad_ref, joined_ref
):
    sides, nodes, width = self_ref.shape
    activated, slope = gelu_parts(pre_ref[...])
    scale = lax.rsqrt(sums_ref[:, 0:1] + epsilon)
    cross = sums_ref[:, 1:2]
    emb_ref[...] = activated * scale
    grad_act = (
        cotangent_ref[...] * scale
        - activated * (cross * scale * scale * scale)
        + (2.0 * penalty_rate / node_total) * activated
    )
    grad = (grad_act * slope).astype(bf16)
    wb_grad_ref[...] = jnp.sum(grad.astype(f32), axis=0, keepdims=True)
    for m in range(sides):
        at = m * width
        w_grad_ref[at : at + width, :] = dot(self_ref[m], grad, (0, 0)).astype(w_grad_ref.dtype)
        joined_ref[0, m] = dot(grad, w_ref[at : at + width, :], (1, 1)).astype(joined_ref.dtype)
    for m in range(sides):
        at = (sides + m) * width
        w_grad_ref[at : at + width, :] = dot(pooled_ref[m], grad, (1, 0)).astype(w_grad_ref.dtype)
        joined_ref[1, m] = dot(grad, w_ref[at : at + width, :], (1, 1)).astype(joined_ref.dtype)


def combine_back(node_total, pre, sums, cotangent, self4, pooled4, w_low):
    nodes, columns = cotangent.shape
    sides, _, width = self4.shape
    return pl.pallas_call(
        functools.partial(combine_back_kernel, node_total),
        out_shape=(
            jax.ShapeDtypeStruct((nodes, columns), f32),
            jax.ShapeDtypeStruct(w_low.shape, f32),
            jax.ShapeDtypeStruct((1, columns), f32),
            jax.ShapeDtypeStruct((2, sides, nodes, width), bf16),
        ),
        compiler_params=params(),
        name="combine_back",
    )(pre, sums, cotangent, self4, pooled4, w_low)


def rows_back_kernel(matrix_ref, pooled_ref, slope_ref, table_ref, grad_ref, q_grad_ref, qb_grad_ref, total_ref):
    step = pl.program_id(0)
    sides, _, width = table_ref.shape
    grad = dot(matrix_ref[...], pooled_ref[...], (1, 0)) * slope_ref[...].astype(f32)
    column_sums = jnp.sum(grad, axis=0, keepdims=True)
    grad = grad.astype(bf16)
    grad_ref[...] = grad

    @pl.when(step == 0)
    def _():
        qb_grad_ref[...] = column_sums
        total_ref[...] = jnp.zeros_like(total_ref)

    @pl.when(step > 0)
    def _():
        qb_grad_ref[...] += column_sums

    for m in range(sides):
        total_ref[:, m * width : (m + 1) * width] += dot(grad, table_ref[m], (0, 0))

    @pl.when(step == pl.num_programs(0) - 1)
    def _():
        q_grad_ref[...] = total_ref[...].T


def rows_back(matrix, grad_pooled, slope, table4):
    sides, row_dev, width = table4.shape
    nodes = matrix.shape[1]
    columns = slope.shape[1]
    block = min(row_dev, 512 * 2048 // nodes)
    return pl.pallas_call(
        rows_back_kernel,
        grid=(row_dev // block,),
        in_specs=[
            pl.BlockSpec((block, nodes), lambda i: (i, 0)),
            pl.BlockSpec(grad_pooled.shape, lambda i: (0, 0)),
            pl.BlockSpec((block, columns), lambda i: (i, 0)),
            pl.BlockSpec((sides, block, width), lambda i: (0, i, 0)),
        ],
        out_specs=(
            pl.BlockSpec((block, columns), lambda i: (i, 0)),
            pl.BlockSpec((sides * width, columns), lambda i: (0, 0)),
            pl.BlockSpec((1, columns), lambda i: (0, 0)),
        ),
        out_shape=(
            jax.ShapeDtypeStruct((row_dev, columns), bf16),
            jax.ShapeDtypeStruct((sides * width, columns), f32),
            jax.ShapeDtypeStruct((1, columns), f32),
        ),
        scratch_shapes=[pltpu.VMEM((columns, sides * width), f32)],
        compiler_params=params(),
        name="rows_back",
    )(matrix, grad_pooled, slope, table4)


def table_back_kernel(grad_ref, q_ref, self_ref, out_ref):
    total = dot(grad_ref[0], q_ref[0], (1, 1))
    for m in range(1, grad_ref.shape[0]):
        total = total + dot(grad_ref[m], q_ref[m], (1, 1))
    out_ref[...] = total

    @pl.when(pl.program_id(0) == 0)
    def _():
        out_ref[0 : self_ref.shape[0], :] += self_ref[...].astype(f32)


def table_back(grad4, q_rows, grad_self):
    sides, row_dev, columns = grad4.shape
    width = q_rows.shape[1]
    block = min(row_dev, 512)
    return pl.pallas_call(
        table_back_kernel,
        grid=(row_dev // block,),
        in_specs=[
            pl.BlockSpec((sides, block, columns), lambda i: (0, i, 0)),
            pl.BlockSpec(q_rows.shape, lambda i: (0, 0, 0)),
            pl.BlockSpec(grad_self.shape, lambda i: (0, 0)),
        ],
        out_specs=pl.BlockSpec((block, width), lambda i: (i, 0)),
        out_shape=jax.ShapeDtypeStruct((row_dev, width), f32),
        compiler_params=params(),
        name="table_back",
    )(grad4, q_rows, grad_self)


def shards(table, q_weight, q_bias, w_weight, w_bias, neighbours, counts, importance, cotangent):
    groups = lax.axis_size("dp")
    sides = lax.axis_size("mp")
    row_dev, width = table.shape
    node_dev, slots_node = neighbours.shape
    node_total = node_dev * groups
    columns = q_weight.shape[1]

    present = jnp.arange(slots_node, dtype=jnp.int32)[None, :] < counts[:, None]
    raw_weights = jnp.where(present, importance, 0.0)
    weights = raw_weights / jnp.sum(raw_weights, axis=1, keepdims=True)
    slots = lax.all_gather(jnp.stack([neighbours.astype(f32).T, weights.T]), "dp")
    table4 = lax.all_gather(table.astype(bf16), "mp")
    q_low = q_weight.astype(bf16)
    w_low = w_weight.astype(bf16)
    q_rows = lax.all_to_all(q_low.reshape(sides, width, columns), "mp", split_axis=0, concat_axis=0, tiled=True)

    base = (lax.axis_index("dp") * row_dev).astype(jnp.int32).reshape(1)
    matrix = spread(base, slots, row_dev)
    slope, pooled_part = pool(table4, q_low, q_bias, matrix, node_dev)
    pooled = lax.psum_scatter(pooled_part, "dp", scatter_dimension=0)
    pooled4 = lax.all_gather(pooled, "mp")
    self4 = table4[:, :node_dev]
    pre, sums = combine(self4, pooled4, w_low, w_bias, cotangent)
    sums = lax.psum(sums, "mp")
    embedding, w_grad, wb_grad, joined_part = combine_back(node_total, pre, sums, cotangent, self4, pooled4, w_low)
    grad_pooled = lax.psum_scatter(joined_part[1], "mp", scatter_dimension=0)
    grad_self = lax.psum_scatter(joined_part[0], "mp", scatter_dimension=0)
    grad_pooled = lax.all_gather(grad_pooled, "dp", axis=0, tiled=True)
    grad, q_grad, qb_grad = rows_back(matrix, grad_pooled, slope, table4)
    grad4 = lax.all_gather(grad, "mp")
    table_grad = table_back(grad4, q_rows, grad_self)
    q_grad, qb_grad, w_grad, wb_grad, square_total = lax.psum(
        (q_grad, qb_grad[0], w_grad, wb_grad[0], jnp.sum(sums[:, 0])), "dp"
    )
    penalty = penalty_rate * square_total / node_total
    return (embedding, table_grad, q_grad, qb_grad, w_grad, wb_grad, penalty)


def solution(mesh):
    placed = (
        P("dp", "mp"),
        P(None, "mp"),
        P("mp"),
        P(None, "mp"),
        P("mp"),
        P("dp", None),
        P("dp"),
        P("dp", None),
        P("dp", "mp"),
    )
    return jax.shard_map(
        shards,
        mesh=mesh,
        in_specs=placed,
        out_specs=(
            P("dp", "mp"),
            P("dp", "mp"),
            P(None, "mp"),
            P("mp"),
            P(None, "mp"),
            P("mp"),
            P(),
        ),
        check_vma=False,
    )
```

```python
import functools

import jax
import jax.numpy as jnp
from jax import lax
from jax.experimental import pallas as pl
from jax.experimental.pallas import tpu as pltpu
from jax.sharding import PartitionSpec as P

epsilon = 1e-06
penalty_rate = 0.01
bf16, f32, i32, i16 = jnp.bfloat16, jnp.float32, jnp.int32, jnp.int16
bucket_rows = 256
lane_tile = 128
weight_unit = 32767.0
code_step = 64
extra_rows = 16
mib = 1024 * 1024
expected_us = dict(
    slots=3,
    low=4,
    spread=20,
    hidden_both=1,
    hidden_slope=5,
    pool=5,
    self_half=3,
    combine=4,
    w_back=4,
    add=2,
    add_pairs=2,
    collect=2,
    stack=1,
    widen=2,
    rows_back_q=13,
    rows_back=9,
    table_back=8,
)


def dot(a, b, contract):
    return lax.dot_general(a, b, ((contract[:1], contract[1:]), ((), ())), preferred_element_type=f32)


def gelu_parts(values):
    c = 0.7978845608028654
    squared = values * values
    t = jnp.tanh(c * values * (1.0 + 0.044715 * squared))
    half = 0.5 * (1.0 + t)
    slope = half + 0.5 * values * (1.0 - t * t) * (c * (1.0 + 3 * 0.044715 * squared))
    return values * half, slope


def size(dims, dtype):
    rows = dims[-2] if len(dims) > 1 else 1
    rest = 1
    for d in dims[:-2]:
        rest *= d
    return rest * (-(-rows // 16) * 16) * (-(-dims[-1] // 128) * 128) * jnp.dtype(dtype).itemsize


def far(array):
    return pltpu.with_memory_space_constraint(array, pltpu.HBM)


def far_shape(dims, dtype):
    return pltpu.HBM(dims, dtype)


def call(kernel, name, operands, outs, grid=(1,), scratch=(), after=(), spare=8):
    specs, arrays, need = [], [], 0
    for operand in operands:
        array, spec = operand if isinstance(operand, tuple) else (operand, whole(operand))
        specs.append(spec)
        arrays.append(array)
        if spec is not smem:
            need += (2 if isinstance(operand, tuple) else 1) * size(spec.block_shape, array.dtype)
    for spec, out in outs:
        need += 2 * size(spec.block_shape, out.dtype)
    for item in scratch:
        need += size(item.shape, item.dtype)
    count = len(arrays)
    inner = lambda *refs: kernel(*refs[:count], *refs[count + len(after) :])
    return pl.pallas_call(
        inner,
        grid=grid,
        in_specs=specs + [pl.BlockSpec(memory_space=pl.ANY)] * len(after),
        out_specs=[o[0] for o in outs],
        out_shape=[o[1] for o in outs],
        scratch_shapes=list(scratch),
        compiler_params=pltpu.CompilerParams(vmem_limit_bytes=need + spare * mib),
        cost_estimate=pl.CostEstimate(
            flops=int(expected_us[name] * 1.15e9), bytes_accessed=int(expected_us[name] * 3.69e6), transcendentals=0
        ),
        name=name,
    )(*arrays, *after)


def full(dims, dtype, kind=jax.ShapeDtypeStruct):
    return whole(shape(dims, dtype)), kind(dims, dtype)


def shape(dims, dtype):
    return jax.ShapeDtypeStruct(dims, dtype)


def whole(array):
    return pl.BlockSpec(array.shape, lambda *_: (0,) * array.ndim)


smem = pl.BlockSpec(memory_space=pltpu.SMEM)


def swap(array, axis, bits):
    size = lax.axis_size(axis)
    return lax.ppermute(array, axis, [(i, i ^ bits) for i in range(size)])


def halves(values):
    high = values.astype(bf16)
    return high, (values - high.astype(f32)).astype(bf16)


def exchange(array, axes):
    return lax.all_to_all(array, axes, split_axis=0, concat_axis=0, tiled=True)


def rows_at(ref, start, size):
    return ref.at[pl.ds(pl.multiple_of(start, size), size)]


def row_blocks(block, columns):
    return pl.BlockSpec((block, columns), lambda i: (i, 0))


def chunk_spec(block, columns, first, count):
    return pl.BlockSpec((block, columns), lambda i: (jnp.clip(i - first, 0, count - 1), 0))


def chunk_specs(chunks, block):
    specs, first = [], 0
    for a in chunks:
        count = a.shape[0] // block
        specs.append(chunk_spec(block, a.shape[1], first, count))
        first += count
    return specs


def low_kernel(first, table_ref, q_ref, w_ref, a_ref, b_ref, q_low_ref, self_ref, pooled_ref):
    step = pl.program_id(0)
    low = table_ref[...].astype(bf16)
    q_low_ref[...] = q_ref[...].astype(bf16)
    w_low = w_ref[...].astype(bf16)

    @pl.when(step < first)
    def _():
        a_ref[...] = low

    @pl.when(step >= first)
    def _():
        b_ref[...] = low

    @pl.when(step < 2)
    def _():
        self_ref[...] = w_low

    @pl.when(step >= 2)
    def _():
        pooled_ref[...] = w_low


def low_all(table, q_weight, w_weight, cut):
    rows, columns = table.shape
    block = rows // 4
    first = cut // block
    q_rows, w_rows = q_weight.shape[0], w_weight.shape[0]
    return call(
        functools.partial(low_kernel, first),
        "low",
        [
            (far(table), row_blocks(block, columns)),
            (far(q_weight), row_blocks(q_rows // 4, columns)),
            (far(w_weight), row_blocks(w_rows // 4, columns)),
        ],
        [
            (chunk_spec(block, columns, 0, first), far_shape((cut, columns), bf16)),
            (chunk_spec(block, columns, first, 4 - first), far_shape((rows - cut, columns), bf16)),
            (row_blocks(q_rows // 4, columns), far_shape((q_rows, columns), bf16)),
            (chunk_spec(w_rows // 4, columns, 0, 2), far_shape((w_rows // 2, columns), bf16)),
            (chunk_spec(w_rows // 4, columns, 2, 2), far_shape((w_rows // 2, columns), bf16)),
        ],
        grid=(4,),
    )


def gate_kernel(*refs):
    del refs


def gate(array, after):
    return pl.pallas_call(
        gate_kernel,
        in_specs=[pl.BlockSpec(memory_space=pl.ANY)] * (1 + len(after)),
        out_specs=pl.BlockSpec(memory_space=pl.ANY),
        out_shape=shape(array.shape, array.dtype),
        input_output_aliases={0: 0},
        compiler_params=pltpu.CompilerParams(vmem_limit_bytes=mib),
        cost_estimate=pl.CostEstimate(flops=1, bytes_accessed=1, transcendentals=0),
        name="gate",
    )(far(array), *map(far, after))


def slots_kernel(row_dev, place_ref, ids_ref, counts_ref, importance_ref, out_ref):
    del place_ref
    ids = ids_ref[...]
    index = lax.broadcasted_iota(i32, ids.shape, 0)
    raw = jnp.where(index < counts_ref[...], importance_ref[...], 0.0)
    weight = raw / jnp.sum(raw, axis=0, keepdims=True)
    bucket = jnp.where(weight > 0.0, ids // bucket_rows, -1)
    within = ids - (ids // bucket_rows) * bucket_rows
    merged = jnp.zeros_like(weight)
    rank = jnp.zeros_like(bucket)
    for k in range(ids.shape[0]):
        merged = merged + jnp.where(ids == ids[k : k + 1, :], weight[k : k + 1, :], 0.0)
        rank = rank + jnp.where((bucket == bucket[k : k + 1, :]) & (index > k), 1, 0)
    amount = jnp.round(merged * weight_unit).astype(i32)
    per = row_dev // bucket_rows
    for d in range(out_ref.shape[0]):
        mine = (bucket >= d * per) & (bucket < (d + 1) * per)
        out_ref[d, 0] = jnp.where(mine, (bucket - d * per) * code_step + rank, -1).astype(i16)
        out_ref[d, 1] = within.astype(i16)
        out_ref[d, 2] = amount.astype(i16)


def make_slots(place, neighbours, counts, importance, row_dev, groups, after=()):
    node_dev, slots_node = neighbours.shape
    return call(
        functools.partial(slots_kernel, row_dev),
        "slots",
        [(place, smem), far(neighbours.T), far(counts.reshape(1, node_dev)), far(importance.T)],
        [full((groups, 3, slots_node, node_dev), i16)],
        after=after,
    )[0]


def spread_kernel(slots_ref, out_ref, all_ref, row_ref, amount_ref):
    _, _, slots_node, lanes = slots_ref.shape
    buckets = out_ref.shape[1] // bucket_rows
    tiles = lanes // lane_tile
    codes = slots_ref[0, 0].astype(i32)
    depth = jnp.max(jnp.where(codes >= 0, (codes & (code_step - 1)) + 1, 0).astype(f32)).astype(i32)
    for t in range(tiles):
        at = slice(t * lane_tile, (t + 1) * lane_tile)
        all_ref[t, 0] = codes[:, at].astype(f32)
        all_ref[t, 1] = slots_ref[0, 1, :, at].astype(i32).astype(f32)
        all_ref[t, 2] = slots_ref[0, 2, :, at].astype(i32).astype(f32) * (1.0 / weight_unit)
    eight = lax.broadcasted_iota(i32, (8, lane_tile), 0).astype(f32)

    def extract(t, first):
        target = eight + first
        for start in range(0, buckets, 8):
            some = range(start, min(start + 8, buckets))
            rows = [jnp.full((8, lane_tile), -1.0, f32) for _ in some]
            amounts = [jnp.zeros((8, lane_tile), f32) for _ in some]
            for k in range(slots_node):
                code = jnp.broadcast_to(all_ref[t, 0, k : k + 1, :], (8, lane_tile))
                row = jnp.broadcast_to(all_ref[t, 1, k : k + 1, :], (8, lane_tile))
                amount = jnp.broadcast_to(all_ref[t, 2, k : k + 1, :], (8, lane_tile))
                for i, b in enumerate(some):
                    hit = code == target + float(b * code_step)
                    rows[i] = jnp.where(hit, row, rows[i])
                    amounts[i] = jnp.where(hit, amount, amounts[i])
            for i, b in enumerate(some):
                row_ref[t, b] = rows[i]
                amount_ref[t, b] = amounts[i]

    tall = (bucket_rows // 16, 16, lane_tile)
    row_index = (lax.broadcasted_iota(i32, tall, 0) * 16 + lax.broadcasted_iota(i32, tall, 1)).astype(f32).astype(bf16)

    def place_all(count, add):
        def one(b, carry):
            at = pl.ds(pl.multiple_of(b * bucket_rows, bucket_rows), bucket_rows)
            for t in range(tiles):
                lane = slice(t * lane_tile, (t + 1) * lane_tile)
                total = out_ref[0, at, lane].reshape(tall) if add else jnp.zeros(tall, bf16)
                for j in range(count):
                    row = jnp.broadcast_to(row_ref[t, b, j : j + 1, :], tall[1:]).astype(bf16)
                    amount = jnp.broadcast_to(amount_ref[t, b, j : j + 1, :], tall[1:]).astype(bf16)
                    total = jnp.where(row_index == row[None], amount[None], total)
                out_ref[0, at, lane] = total.reshape(bucket_rows, lane_tile)
            return carry

        lax.fori_loop(0, buckets, one, 0)

    for t in range(tiles):
        extract(t, 0.0)
    for low, high in ((0, 3), (4, 4), (5, 5), (6, 6), (7, slots_node)):

        @pl.when((depth >= low) & (depth <= high))
        def _():
            place_all(min(high, 8), False)

    def more(p, carry):
        for t in range(tiles):
            extract(t, (p * 8).astype(f32))
        place_all(8, True)
        return carry

    lax.fori_loop(1, (depth + 7) // 8, more, 0)


def spread(slots, row_dev):
    groups, _, slots_node, node_dev = slots.shape
    tiles = node_dev // lane_tile
    buckets = row_dev // bucket_rows
    return call(
        spread_kernel,
        "spread",
        [(slots, pl.BlockSpec((1, 3, slots_node, node_dev), lambda i: (i, 0, 0, 0)))],
        [(pl.BlockSpec((1, row_dev, node_dev), lambda i: (i, 0, 0)), shape((groups, row_dev, node_dev), bf16))],
        grid=(groups,),
        scratch=[
            pltpu.VMEM((tiles, 3, slots_node, lane_tile), f32),
            pltpu.VMEM((tiles, buckets, 8, lane_tile), f32),
            pltpu.VMEM((tiles, buckets, 8, lane_tile), f32),
        ],
    )[0]


def hidden_kernel(sides, want, place_ref, *refs):
    table, q_ref, bias_ref, outs = refs[:sides], refs[sides], refs[sides + 1], refs[sides + 2 :]
    width = table[0].shape[1]
    pre = bias_ref[...]
    for j in range(sides):
        pre = pre + dot(table[j][...], rows_at(q_ref, (place_ref[1] ^ j) * width, width)[...], (1, 0))
    value, slope = gelu_parts(pre)
    if want == "both":
        outs[0][...] = value.astype(bf16).T
    outs[-1][...] = slope.astype(bf16)


def hidden(place, table, q_low, bias, want, after=()):
    rows, width = table[0].shape
    columns = q_low.shape[1]
    sides = len(table)
    block = min(rows, 512)
    outs = [(row_blocks(block, columns), far_shape((rows, columns), bf16))]
    if want == "both":
        outs.insert(0, (pl.BlockSpec((columns, block), lambda i: (0, i)), shape((columns, rows), bf16)))
    return call(
        functools.partial(hidden_kernel, sides, want),
        "hidden_" + want,
        [(place, smem)]
        + [(far(a), row_blocks(block, width)) for a in table]
        + [far(q_low), far(bias.reshape(1, columns))],
        outs,
        grid=(rows // block,),
        after=after,
    )


def pool_kernel(last, hidden_ref, matrix_ref, *refs):
    for g in range(matrix_ref.shape[0]):
        total = dot(hidden_ref[...], matrix_ref[g], (1, 0))
        nodes = total.shape[1]
        at = slice(g * nodes, (g + 1) * nodes)
        if last:
            refs[1][at, :] = (refs[0][:, at] + total).T.astype(bf16)
        else:
            refs[0][:, at] = total


def pool(hidden_t, matrix, first, so_far, after=()):
    columns, rows = hidden_t.shape
    groups, _, node_dev = matrix.shape
    nodes = groups * node_dev
    last = so_far is not None
    total_block = pl.BlockSpec((columns, 2 * node_dev), lambda i: (0, i))
    return call(
        functools.partial(pool_kernel, last),
        "pool",
        [hidden_t, (matrix, pl.BlockSpec((2, rows, node_dev), lambda i: (i, first // rows, 0)))]
        + ([(so_far, total_block)] if last else []),
        [
            (row_blocks(2 * node_dev, columns), shape((nodes, columns), bf16))
            if last
            else (total_block, shape((columns, nodes), f32))
        ],
        grid=(groups // 2,),
        after=after,
    )[0]


def first_rows(table, nodes):
    return [(far(a), pl.BlockSpec((nodes, a.shape[1]), lambda *_: (0, 0))) for a in table]


def self_kernel(sides, place_ref, *refs):
    own, (w_ref, bias_ref, cotangent_ref), outs = refs[:sides], refs[sides : sides + 3], refs[sides + 3 : -1]
    pre_ref = refs[-1]
    width = own[0].shape[1]
    pre = bias_ref[...]
    for j in range(sides):
        pre = pre + dot(own[j][...], rows_at(w_ref, (place_ref[1] ^ j) * width, width)[...], (1, 0))
    pre_ref[...] = pre
    few, columns = outs[0].shape[0], pre.shape[1]
    for j in range(sides):
        at = (place_ref[1] ^ j) * few
        outs[j][:, 0:columns] = rows_at(pre_ref, at, few)[...]
        outs[j][:, columns:] = rows_at(cotangent_ref, at, few)[...]


def self_half(place, table, w_self, bias, cotangent, after=()):
    nodes, columns = cotangent.shape
    sides = len(table)
    return call(
        functools.partial(self_kernel, sides),
        "self_half",
        [(place, smem)] + first_rows(table, nodes) + [far(w_self), far(bias.reshape(1, columns)), far(cotangent)],
        [full((nodes // sides, 2 * columns), f32, far_shape)] * sides,
        scratch=[pltpu.VMEM((nodes, columns), f32)],
        after=after,
    )


def combine_kernel(node_total, sides, parts_ref, *refs):
    early, w_refs = refs[:sides], refs[sides : 2 * sides]
    grad_ref, late = refs[2 * sides], refs[2 * sides + 1 :]
    groups, _, few, columns = parts_ref.shape
    pooled = []
    for m in range(sides):
        total = parts_ref[0, m].astype(f32)
        for g in range(1, groups):
            total = total + parts_ref[g, m].astype(f32)
        pooled.append(total.astype(bf16))
    pooled = jnp.concatenate(pooled, axis=1)
    activated, slope, squares, cross = [], [], 0.0, 0.0
    for j in range(sides):
        pre = early[j][:, 0:columns] + dot(pooled, w_refs[j][...], (1, 0))
        a, s = gelu_parts(pre)
        activated.append(a)
        slope.append(s)
        squares = squares + jnp.sum(a * a, axis=1, keepdims=True)
        cross = cross + jnp.sum(a * early[j][:, columns:], axis=1, keepdims=True)
    scale = lax.rsqrt(squares + epsilon)
    pull = cross * scale * scale * scale
    grad_pooled = 0.0
    square_high, square_low = halves(jnp.sum(squares, axis=0, keepdims=True))
    index = lax.broadcasted_iota(i32, (extra_rows, late[0].shape[1]), 0)
    extra = jnp.where(
        index == 0, square_high.astype(f32), jnp.where(index == 1, square_low.astype(f32), 0.0)
    ).astype(bf16)
    for j in range(sides):
        grad_act = early[j][:, columns:] * scale - activated[j] * pull + (2.0 * penalty_rate / node_total) * activated[j]
        grad = (grad_act * slope[j]).astype(bf16)
        grad_pooled = grad_pooled + dot(grad, w_refs[j][...], (1, 1))
        high, low = halves(activated[j] * scale)
        late[j][0:few, 0:columns] = high
        late[j][0:few, columns : 2 * columns] = low
        late[j][0:few, 2 * columns : 3 * columns] = grad
        late[j][0:few, 3 * columns :] = pooled
        late[j][few:, :] = extra
    for m in range(sides):
        part = grad_pooled[:, m * columns : (m + 1) * columns].astype(bf16)
        for g in range(groups):
            grad_ref[g, m] = part


def combine(node_total, parts, early, w_pooled, after=()):
    groups, sides, few, columns = parts.shape
    return call(
        functools.partial(combine_kernel, node_total, sides),
        "combine",
        [parts, *map(far, early), *map(far, w_pooled)],
        [full(parts.shape, bf16)] + [full((few + extra_rows, (3 + sides) * columns), bf16, far_shape)] * sides,
        after=after,
    )


def w_back_kernel(sides, groups, place_ref, *refs):
    own, late, (w_ref, emb_ref, even_ref, odd_ref, *self_refs), scratch = (
        refs[:sides],
        refs[sides : 2 * sides],
        refs[2 * sides : -3],
        refs[-3:],
    )
    grad_ref, pooled_ref, total_ref = scratch
    nodes, columns = emb_ref.shape
    few = nodes // sides
    squares = 0.0
    for j in range(sides):
        at = (place_ref[1] ^ j) * few
        rows_at(emb_ref, at, few)[...] = late[j][0:few, 0:columns].astype(f32) + late[j][
            0:few, columns : 2 * columns
        ].astype(f32)
        rows_at(grad_ref, at, few)[...] = late[j][0:few, 2 * columns : 3 * columns]
        rows_at(pooled_ref, at, few)[...] = late[j][0:few, 3 * columns :]
        squares = squares + late[j][few : few + 1, 0:columns].astype(f32)
        squares = squares + late[j][few + 1 : few + 2, 0:columns].astype(f32)
    grad = grad_ref[...]
    for j in range(sides):
        side = place_ref[1] ^ j
        rows_at(total_ref, side * columns, columns)[...] = dot(own[j][...], grad, (0, 0))
        self_refs[j][...] = dot(grad, rows_at(w_ref, side * columns, columns)[...], (1, 1)).astype(bf16)
    total_ref[sides * columns :, :] = dot(pooled_ref[...], grad, (0, 0))
    bias_high, bias_low = halves(jnp.sum(grad.astype(f32), axis=0, keepdims=True))
    square_high, square_low = halves(squares)
    piece = total_ref.shape[0] // groups
    index = lax.broadcasted_iota(i32, (extra_rows, columns), 0)
    extra = jnp.zeros(index.shape, f32)
    for i, row in enumerate((bias_high, bias_low, square_high, square_low)):
        extra = jnp.where(index == i, row.astype(f32), extra)
    extra = extra.astype(bf16)
    for s in range(groups):
        part = (odd_ref if s % 2 else even_ref).at[s // 2]
        part[0:piece, :] = rows_at(total_ref, (place_ref[0] ^ s) * piece, piece)[...].astype(bf16)
        part[piece:, :] = extra


def w_back(place, table, late, w_self, node_dev, groups, after=()):
    sides = len(table)
    rows, columns = 2 * w_self.shape[0], w_self.shape[1]
    half = full((groups // 2, rows // groups + extra_rows, columns), bf16, far_shape)
    return call(
        functools.partial(w_back_kernel, sides, groups),
        "w_back",
        [(place, smem)] + first_rows(table, node_dev) + [*map(far, late), far(w_self)],
        [full((node_dev, columns), f32, far_shape), half, half]
        + [full((node_dev, columns), bf16, far_shape)] * sides,
        scratch=[
            pltpu.VMEM((node_dev, columns), bf16),
            pltpu.VMEM((node_dev, sides * columns), bf16),
            pltpu.VMEM((rows, columns), f32),
        ],
        after=after,
    )


def split_extra(total):
    index = lax.broadcasted_iota(i32, total.shape, 0)
    extra = jnp.zeros(total.shape, f32)
    for i in (0, 2):
        high, low = halves(total[i : i + 1, :] + total[i + 1 : i + 2, :])
        extra = jnp.where(index == i, high.astype(f32), jnp.where(index == i + 1, low.astype(f32), extra))
    return extra


def add_kernel(copies, scale, count, *refs):
    parts, (piece_ref, bias_ref, scalar_ref) = refs[:count], refs[count:]
    terms = []
    for part in parts:
        terms += [part] if len(part.shape) == 2 else [part.at[i] for i in range(part.shape[0])]
    total = terms[0][...].astype(f32)
    for part in terms[1:]:
        total = total + part[...].astype(f32)
    piece = total.shape[0] - extra_rows
    low = total[0:piece, :].astype(bf16)
    if copies:
        for i in range(copies):
            piece_ref[i] = low
    else:
        piece_ref[...] = low
    bias_ref[...] = total[piece : piece + 1, :] + total[piece + 1 : piece + 2, :]
    scalar_ref[...] = scale * (total[piece + 2 : piece + 3, 0:1] + total[piece + 3 : piece + 4, 0:1])


def add(parts, copies, scale):
    rows, columns = parts[0].shape[-2:]
    piece = (rows - extra_rows, columns)
    return call(
        functools.partial(add_kernel, copies, scale, len(parts)),
        "add",
        parts,
        [full((copies, *piece) if copies else piece, bf16), full((1, columns), f32), full((1, 1), f32)],
    )


def add_pairs_kernel(own_ref, other_ref, *outs):
    for i, out in enumerate(outs):
        total = own_ref[i].astype(f32) + other_ref[i].astype(f32)
        piece = total.shape[0] - extra_rows
        out[0:piece, :] = total[0:piece, :].astype(bf16)
        out[piece:, :] = split_extra(total[piece:, :]).astype(bf16)


def add_pairs(own, other, after=()):
    count, rows, columns = own.shape
    return call(add_pairs_kernel, "add_pairs", [far(own), far(other)], [full((rows, columns), bf16, far_shape)] * count, after=after)


def stack_kernel(*refs):
    for i, ref in enumerate(refs[:-1]):
        refs[-1][i] = ref[...]


def stack(arrays):
    return call(stack_kernel, "stack", arrays, [full((len(arrays), *arrays[0].shape), bf16)])[0]


def collect_kernel(place_ref, own_ref, other_ref, out_ref):
    count, piece, _ = other_ref.shape
    for s in range(count):
        rows_at(out_ref, (place_ref[0] ^ (2 * s)) * piece, piece)[...] = own_ref[s].astype(f32)
        rows_at(out_ref, (place_ref[0] ^ (2 * s + 1)) * piece, piece)[...] = other_ref[s].astype(f32)


def collect(place, own, other):
    count, piece, columns = own.shape
    return call(
        collect_kernel, "collect", [(place, smem), own, other], [full((2 * count * piece, columns), f32)]
    )[0]


def widen_kernel(low_ref, out_ref):
    out_ref[...] = low_ref[...].astype(f32)


def widen(low):
    rows, columns = low.shape
    block = rows // 2
    return call(
        widen_kernel,
        "widen",
        [(low, row_blocks(block, columns))],
        [(row_blocks(block, columns), shape((rows, columns), f32))],
        grid=(2,),
    )[0]


def total_direct(parts, scale=0.0):
    groups, rows, columns = parts.shape
    pieces, *sums = add([exchange(parts, "dp")], groups, scale)
    return widen(exchange(pieces, "dp").reshape(-1, columns)), *sums


def total_in_steps(place, parts, scale, after=()):
    count = parts[0].shape[0]
    mine = add_pairs(parts[0], swap(parts[1], "dp", 1), after=after)
    piece, *sums = add([mine[0]] + [swap(mine[s], "dp", 2 * s) for s in range(1, count)], 0, scale)
    pieces = stack([piece] + [swap(piece, "dp", 2 * s) for s in range(1, count)])
    return collect(place, pieces, swap(pieces, "dp", 1)), *sums


def rows_back_kernel(chunk_counts, sides, place_ref, *refs):
    chunks = len(chunk_counts)
    matrix_ref, pooled_ref, slopes = refs[0], refs[1], refs[2 : 2 + chunks]
    table = refs[2 + chunks : 2 + chunks + chunks * sides]
    grad_ref, rest = refs[2 + chunks + chunks * sides], refs[3 + chunks + chunks * sides :]
    step = pl.program_id(0)
    matrix = jnp.concatenate([matrix_ref[g] for g in range(matrix_ref.shape[0])], axis=1)
    summed = dot(matrix, pooled_ref[...], (1, 0))
    slope = slopes[0][...]
    first = chunk_counts[0]
    for k in range(1, chunks):
        slope = jnp.where(step >= first, slopes[k][...], slope)
        first += chunk_counts[k]
    grad = summed * slope.astype(f32)
    column_sums = jnp.sum(grad, axis=0, keepdims=True)
    grad = grad.astype(bf16)
    grad_ref[...] = grad
    if not sides:
        return
    q_ref, total_ref, bias_ref = rest
    width = table[0].shape[1]

    @pl.when(step == 0)
    def _():
        bias_ref[...] = jnp.zeros_like(bias_ref)
        total_ref[...] = jnp.zeros_like(total_ref)

    bias_ref[...] += column_sums
    first = 0
    for k in range(chunks):

        @pl.when((step >= first) & (step < first + chunk_counts[k]))
        def _():
            for j in range(sides):
                total_ref[j] += dot(grad, table[k * sides + j][...], (0, 0))

        first += chunk_counts[k]

    @pl.when(step == pl.num_programs(0) - 1)
    def _():
        high, low = halves(bias_ref[...])
        groups, rows, columns = q_ref.shape
        index = lax.broadcasted_iota(i32, (extra_rows, columns), 0)
        extra = jnp.where(index == 0, high.astype(f32), jnp.where(index == 1, low.astype(f32), 0.0)).astype(bf16)
        piece = rows - extra_rows
        per = width // piece
        for g in range(groups):
            q_ref[g, piece:, :] = extra
        for j in range(sides):
            flat = total_ref[j].T.astype(bf16)
            for part in range(per):
                q_ref[(place_ref[1] ^ j) * per + part, 0:piece, :] = flat[part * piece : (part + 1) * piece, :]


def rows_back(place, matrix, pooled, slopes, table, after=()):
    sides = len(table[0]) if table else 0
    groups, row_dev, node_dev = matrix.shape
    columns = pooled.shape[1]
    block = min(slopes[-1].shape[0], 512 * 2048 // (groups * node_dev))
    counts = [a.shape[0] // block for a in slopes]
    operands = [(place, smem), (far(matrix), pl.BlockSpec((groups, block, node_dev), lambda i: (0, i, 0))), pooled]
    operands += list(zip(map(far, slopes), chunk_specs(slopes, block)))
    outs = [(row_blocks(block, columns), far_shape((row_dev, columns), bf16))]
    scratch = []
    if sides:
        width = table[0][0].shape[1]
        by_side = [chunk_specs([part[j] for part in table], block) for j in range(sides)]
        operands += [(far(table[k][j]), by_side[j][k]) for k in range(len(table)) for j in range(sides)]
        outs.append(full((groups, sides * width // groups + extra_rows, columns), bf16))
        scratch = [pltpu.VMEM((sides, columns, width), f32), pltpu.VMEM((1, columns), f32)]
    return call(
        functools.partial(rows_back_kernel, counts, sides),
        "rows_back_q" if sides else "rows_back",
        operands,
        outs,
        grid=(row_dev // block,),
        scratch=scratch,
        after=after,
    )


def table_back_kernel(sides, place_ref, *refs):
    grads, qs, self_refs, out_ref = refs[:sides], refs[sides : 2 * sides], refs[2 * sides : 3 * sides], refs[-1]
    width = out_ref.shape[1]
    at = place_ref[1] * width
    total = dot(grads[0][...], rows_at(qs[0], at, width)[...], (1, 1))
    for j in range(1, sides):
        total = total + dot(grads[j][...], rows_at(qs[j], at, width)[...], (1, 1))
    out_ref[...] = total

    @pl.when(pl.program_id(0) == 0)
    def _():
        nodes = self_refs[0].shape[0]
        own = self_refs[0][...].astype(f32)
        for ref in self_refs[1:]:
            own = own + ref[...].astype(f32)
        out_ref[0:nodes, :] += own


def table_back(place, grads, qs, grad_self):
    sides = len(grads)
    row_dev, columns = grads[0].shape
    width = grad_self[0].shape[1]
    block = min(row_dev, 512)
    return call(
        functools.partial(table_back_kernel, sides),
        "table_back",
        [(place, smem)] + [(far(a), row_blocks(block, columns)) for a in grads] + [*map(far, qs), *map(far, grad_self)],
        [(row_blocks(block, width), far_shape((row_dev, width), f32))],
        grid=(row_dev // block,),
    )[0]


def all_sides(array):
    across = swap(array, "mp", 2)
    return [array, swap(array, "mp", 1), across, swap(across, "mp", 1)]


def shards(table, q_weight, q_bias, w_weight, w_bias, neighbours, counts, importance, cotangent):
    groups = lax.axis_size("dp")
    sides = lax.axis_size("mp")
    row_dev, width = table.shape
    node_dev, _ = neighbours.shape
    node_total = node_dev * groups
    columns = q_weight.shape[1]
    few = node_dev // sides
    place = jnp.stack([lax.axis_index("dp"), lax.axis_index("mp")]).astype(i32)

    cut = row_dev * 3 // 4
    low_a, low_b, q_low, w_self, w_pooled = low_all(table, q_weight, w_weight, cut)
    slots = make_slots(place, neighbours, counts, importance, row_dev, groups, after=[low_a])
    slots = exchange(slots, "dp")
    across_a, across_b = swap(low_a, "mp", 2), swap(low_b, "mp", 2)
    beside_a, beside_b = swap(low_a, "mp", 1), swap(low_b, "mp", 1)

    matrix = spread(slots, row_dev)
    across_a = gate(across_a, [matrix])
    part_a = [low_a, beside_a, across_a, swap(across_a, "mp", 1)]
    hidden_a, slope_a = hidden(place, part_a, q_low, q_bias, "both")
    so_far = pool(hidden_a, matrix, 0, None)
    across_b = gate(across_b, [hidden_a])
    part_b = [low_b, beside_b, across_b, swap(across_b, "mp", 1)]
    parts = [part_a, part_b]
    early = self_half(place, part_a, w_self, w_bias, cotangent)
    early = [early[0]] + [swap(early[j], "mp", j) for j in range(1, sides)]
    hidden_b, slope_b = hidden(place, part_b, q_low, q_bias, "both", after=[so_far])
    pooled = pool(hidden_b, matrix, cut, so_far, after=early)
    slope = [slope_a, slope_b]
    pooled = exchange(pooled.reshape(groups * sides, few, columns), ("dp", "mp"))

    w_pooled = all_sides(gate(w_pooled, [hidden_b]))
    q_all = all_sides(gate(q_low, [hidden_b]))
    q_bias_x = swap(q_bias, "mp", 2)
    slope_x = [hidden(place, part, q_all[2], q_bias_x, "slope")[0] for part in parts]

    grad_pooled, *late = combine(
        node_total, pooled.reshape(groups, sides, few, columns), early, w_pooled, after=slope_x
    )
    grad_pooled = exchange(grad_pooled.reshape(groups * sides, few, columns), ("dp", "mp")).reshape(node_total, columns)
    late = [late[0]] + [swap(late[j], "mp", j) for j in range(1, sides)]
    embedding, *w_parts = w_back(place, part_a, late, w_self, node_dev, groups)
    w_parts, grad_self = w_parts[:2], w_parts[2:]
    grad_self = [grad_self[0]] + [swap(grad_self[j], "mp", j) for j in range(1, sides)]

    grad_pooled_x = swap(grad_pooled, "mp", 2)
    grad, q_parts = rows_back(place, matrix, grad_pooled, slope, parts, after=[embedding])
    grad_x = rows_back(place, matrix, grad_pooled_x, slope_x, [], after=[grad])[0]
    grads = [grad, swap(grad, "mp", 1), grad_x, swap(grad_x, "mp", 1)]
    table_grad = table_back(place, grads, q_all, grad_self)
    q_grad, q_bias_grad, _ = total_direct(q_parts)
    scale = penalty_rate / node_total
    if groups <= 8:
        w_grad, w_bias_grad, penalty = total_in_steps(place, w_parts, scale, after=[grad])
    else:
        order = place[0] ^ jnp.arange(groups, dtype=i32)
        w_grad, w_bias_grad, penalty = total_direct(jnp.stack(w_parts)[order % 2, order // 2], scale)
    return (
        embedding,
        table_grad,
        q_grad,
        q_bias_grad.reshape(columns),
        w_grad,
        w_bias_grad.reshape(columns),
        penalty.reshape(()),
    )


def solution(mesh):
    placed = (
        P("dp", "mp"),
        P(None, "mp"),
        P("mp"),
        P(None, "mp"),
        P("mp"),
        P("dp", None),
        P("dp"),
        P("dp", None),
        P("dp", "mp"),
    )
    return jax.shard_map(
        shards,
        mesh=mesh,
        in_specs=placed,
        out_specs=(
            P("dp", "mp"),
            P("dp", "mp"),
            P(None, "mp"),
            P("mp"),
            P(None, "mp"),
            P("mp"),
            P(),
        ),
        check_vma=False,
    )
```

```python
import collections
import functools

import jax
import jax.numpy as jnp
from jax import lax
from jax.experimental import pallas as pl
from jax.experimental.pallas import tpu as pltpu
from jax.sharding import PartitionSpec as P

epsilon = 1e-06
penalty_rate = 0.01
bf16, f32, i32, i16 = jnp.bfloat16, jnp.float32, jnp.int32, jnp.int16
bucket_rows = 256
lane_tile = 128
weight_unit = 32767.0
code_step = 64
extra_rows = 16
mib = 1024 * 1024
expected_us = collections.defaultdict(
    lambda: 0.001,
    hidden_slope=5,
    self_half=3,
    combine=4,
    w_back=4,
    rows_back=16,
    add=20,
    add_some=1,
    add_pairs=2,
    table_back=20,
    cut=1,
    collect=2,
    widen=1,
)


def dot(a, b, contract):
    return lax.dot_general(a, b, ((contract[:1], contract[1:]), ((), ())), preferred_element_type=f32)


def gelu_parts(values):
    c = 0.7978845608028654
    squared = values * values
    t = jnp.tanh(c * values * (1.0 + 0.044715 * squared))
    half = 0.5 * (1.0 + t)
    slope = half + 0.5 * values * (1.0 - t * t) * (c * (1.0 + 3 * 0.044715 * squared))
    return values * half, slope


def size(dims, dtype):
    rows = dims[-2] if len(dims) > 1 else 1
    rest = 1
    for d in dims[:-2]:
        rest *= d
    return rest * (-(-rows // 16) * 16) * (-(-dims[-1] // 128) * 128) * jnp.dtype(dtype).itemsize


def far(array):
    return pltpu.with_memory_space_constraint(array, pltpu.HBM)


def far_shape(dims, dtype):
    return pltpu.HBM(dims, dtype)


def call(kernel, name, operands, outs, grid=(1,), scratch=(), after=(), aliases={}, spare=8):
    specs, arrays, need = [], [], 0
    for operand in operands:
        array, spec = operand if isinstance(operand, tuple) else (operand, whole(operand))
        specs.append(spec)
        arrays.append(array)
        if spec is not smem:
            need += (2 if isinstance(operand, tuple) else 1) * size(spec.block_shape, array.dtype)
    for spec, out in outs:
        need += 2 * size(spec.block_shape, out.dtype)
    for item in scratch:
        need += size(item.shape, item.dtype)
    count = len(arrays)
    inner = lambda *refs: kernel(*refs[:count], *refs[count + len(after) :])
    return pl.pallas_call(
        inner,
        grid=grid,
        in_specs=specs + [pl.BlockSpec(memory_space=pl.ANY)] * len(after),
        out_specs=[o[0] for o in outs],
        out_shape=[o[1] for o in outs],
        scratch_shapes=list(scratch),
        input_output_aliases=dict(aliases),
        compiler_params=pltpu.CompilerParams(vmem_limit_bytes=need + spare * mib),
        cost_estimate=pl.CostEstimate(
            flops=int(expected_us[name] * 1.15e9), bytes_accessed=int(expected_us[name] * 3.69e6), transcendentals=0
        ),
        name=name,
    )(*arrays, *after)


def full(dims, dtype, kind=jax.ShapeDtypeStruct):
    return whole(shape(dims, dtype)), kind(dims, dtype)


def shape(dims, dtype):
    return jax.ShapeDtypeStruct(dims, dtype)


def whole(array):
    return pl.BlockSpec(array.shape, lambda *_: (0,) * array.ndim)


smem = pl.BlockSpec(memory_space=pltpu.SMEM)


def swap(array, axis, bits):
    size = lax.axis_size(axis)
    return lax.ppermute(array, axis, [(i, i ^ bits) for i in range(size)])


def halves(values):
    high = values.astype(bf16)
    return high, (values - high.astype(f32)).astype(bf16)


def exchange(array, axes):
    return lax.all_to_all(array, axes, split_axis=0, concat_axis=0, tiled=True)


def rows_at(ref, start, size):
    return ref.at[pl.ds(pl.multiple_of(start, size), size)]


def row_blocks(block, columns):
    return pl.BlockSpec((block, columns), lambda i: (i, 0))


def chunk_spec(block, columns, first, count):
    return pl.BlockSpec((block, columns), lambda i: (jnp.clip(i - first, 0, count - 1), 0))


def chunk_specs(chunks, block):
    specs, first = [], 0
    for a in chunks:
        count = a.shape[0] // block
        specs.append(chunk_spec(block, a.shape[1], first, count))
        first += count
    return specs


def low_kernel(count, *refs):
    for i in range(count):
        refs[count + i][...] = refs[i][...].astype(bf16)


def low(pieces, after=()):
    steps = 4
    operands, outs = [], []
    for array, first, rows in pieces:
        block, columns = rows // steps, array.shape[1]
        operands.append(
            (far(array), pl.BlockSpec((block, columns), functools.partial(lambda f, i: (f + i, 0), first // block)))
        )
        outs.append((row_blocks(block, columns), far_shape((rows, columns), bf16)))
    return call(functools.partial(low_kernel, len(pieces)), "low", operands, outs, grid=(steps,), after=after)


def gate_kernel(*refs):
    del refs


def gate(array, after):
    return pl.pallas_call(
        gate_kernel,
        in_specs=[pl.BlockSpec(memory_space=pl.ANY)] * (1 + len(after)),
        out_specs=pl.BlockSpec(memory_space=pl.ANY),
        out_shape=shape(array.shape, array.dtype),
        input_output_aliases={0: 0},
        compiler_params=pltpu.CompilerParams(vmem_limit_bytes=mib),
        cost_estimate=pl.CostEstimate(flops=1, bytes_accessed=1, transcendentals=0),
        name="gate",
    )(array, *after)


def slots_kernel(row_dev, place_ref, ids_ref, counts_ref, importance_ref, out_ref):
    del place_ref
    ids = ids_ref[...]
    index = lax.broadcasted_iota(i32, ids.shape, 0)
    raw = jnp.where(index < counts_ref[...], importance_ref[...], 0.0)
    weight = raw / jnp.sum(raw, axis=0, keepdims=True)
    bucket = jnp.where(weight > 0.0, ids // bucket_rows, -1)
    within = ids - (ids // bucket_rows) * bucket_rows
    merged = jnp.zeros_like(weight)
    rank = jnp.zeros_like(bucket)
    for k in range(ids.shape[0]):
        merged = merged + jnp.where(ids == ids[k : k + 1, :], weight[k : k + 1, :], 0.0)
        rank = rank + jnp.where((bucket == bucket[k : k + 1, :]) & (index > k), 1, 0)
    amount = jnp.round(merged * weight_unit).astype(i32)
    per = row_dev // bucket_rows
    for d in range(out_ref.shape[0]):
        mine = (bucket >= d * per) & (bucket < (d + 1) * per)
        out_ref[d, 0] = jnp.where(mine, (bucket - d * per) * code_step + rank, -1).astype(i16)
        out_ref[d, 1] = within.astype(i16)
        out_ref[d, 2] = amount.astype(i16)


def make_slots(place, neighbours, counts, importance, row_dev, groups, after=()):
    node_dev, slots_node = neighbours.shape
    return call(
        functools.partial(slots_kernel, row_dev),
        "slots",
        [(place, smem), far(neighbours.T), far(counts.reshape(1, node_dev)), far(importance.T)],
        [full((groups, 3, slots_node, node_dev), i16)],
        after=after,
    )[0]


def spread_kernel(slots_ref, out_ref, all_ref, row_ref, amount_ref):
    _, _, slots_node, lanes = slots_ref.shape
    buckets = out_ref.shape[1] // bucket_rows
    tiles = lanes // lane_tile
    codes = slots_ref[0, 0].astype(i32)
    depth = jnp.max(jnp.where(codes >= 0, (codes & (code_step - 1)) + 1, 0).astype(f32)).astype(i32)
    for t in range(tiles):
        at = slice(t * lane_tile, (t + 1) * lane_tile)
        all_ref[t, 0] = codes[:, at].astype(f32)
        all_ref[t, 1] = slots_ref[0, 1, :, at].astype(i32).astype(f32)
        all_ref[t, 2] = slots_ref[0, 2, :, at].astype(i32).astype(f32) * (1.0 / weight_unit)
    eight = lax.broadcasted_iota(i32, (8, lane_tile), 0).astype(f32)

    def extract(t, first):
        target = eight + first
        for start in range(0, buckets, 8):
            some = range(start, min(start + 8, buckets))
            rows = [jnp.full((8, lane_tile), -1.0, f32) for _ in some]
            amounts = [jnp.zeros((8, lane_tile), f32) for _ in some]
            for k in range(slots_node):
                code = jnp.broadcast_to(all_ref[t, 0, k : k + 1, :], (8, lane_tile))
                row = jnp.broadcast_to(all_ref[t, 1, k : k + 1, :], (8, lane_tile))
                amount = jnp.broadcast_to(all_ref[t, 2, k : k + 1, :], (8, lane_tile))
                for i, b in enumerate(some):
                    hit = code == target + float(b * code_step)
                    rows[i] = jnp.where(hit, row, rows[i])
                    amounts[i] = jnp.where(hit, amount, amounts[i])
            for i, b in enumerate(some):
                row_ref[t, b] = rows[i]
                amount_ref[t, b] = amounts[i]

    tall = (bucket_rows // 16, 16, lane_tile)
    row_index = (lax.broadcasted_iota(i32, tall, 0) * 16 + lax.broadcasted_iota(i32, tall, 1)).astype(f32).astype(bf16)

    def place_all(count, add):
        def one(b, carry):
            at = pl.ds(pl.multiple_of(b * bucket_rows, bucket_rows), bucket_rows)
            for t in range(tiles):
                lane = slice(t * lane_tile, (t + 1) * lane_tile)
                total = out_ref[0, at, lane].reshape(tall) if add else jnp.zeros(tall, bf16)
                for j in range(count):
                    row = jnp.broadcast_to(row_ref[t, b, j : j + 1, :], tall[1:]).astype(bf16)
                    amount = jnp.broadcast_to(amount_ref[t, b, j : j + 1, :], tall[1:]).astype(bf16)
                    total = jnp.where(row_index == row[None], amount[None], total)
                out_ref[0, at, lane] = total.reshape(bucket_rows, lane_tile)
            return carry

        lax.fori_loop(0, buckets, one, 0)

    for t in range(tiles):
        extract(t, 0.0)
    for low, high in ((0, 3), (4, 4), (5, 5), (6, 6), (7, slots_node)):

        @pl.when((depth >= low) & (depth <= high))
        def _():
            place_all(min(high, 8), False)

    def more(p, carry):
        for t in range(tiles):
            extract(t, (p * 8).astype(f32))
        place_all(8, True)
        return carry

    lax.fori_loop(1, (depth + 7) // 8, more, 0)


def spread(slots, row_dev, after=()):
    groups, _, slots_node, node_dev = slots.shape
    tiles = node_dev // lane_tile
    buckets = row_dev // bucket_rows
    return call(
        spread_kernel,
        "spread",
        [(slots, pl.BlockSpec((1, 3, slots_node, node_dev), lambda i: (i, 0, 0, 0)))],
        [(pl.BlockSpec((1, row_dev, node_dev), lambda i: (i, 0, 0)), shape((groups, row_dev, node_dev), bf16))],
        grid=(groups,),
        scratch=[
            pltpu.VMEM((tiles, 3, slots_node, lane_tile), f32),
            pltpu.VMEM((tiles, buckets, 8, lane_tile), f32),
            pltpu.VMEM((tiles, buckets, 8, lane_tile), f32),
        ],
        after=after,
    )[0]


def hidden_kernel(sides, want, place_ref, *refs):
    table, q_ref, bias_ref, outs = refs[:sides], refs[sides], refs[sides + 1], refs[sides + 2 :]
    width = table[0].shape[1]
    pre = bias_ref[...]
    for j in range(sides):
        pre = pre + dot(table[j][...], rows_at(q_ref, (place_ref[1] ^ j) * width, width)[...], (1, 0))
    value, slope = gelu_parts(pre)
    if want == "value":
        outs[0][...] = value.astype(bf16).T
    else:
        outs[0][...] = slope.astype(bf16)


def hidden(place, table, q_low, bias, want, after=()):
    rows, width = table[0].shape
    columns = q_low.shape[1]
    sides = len(table)
    block = min(rows, 512)
    if want == "value":
        out = (pl.BlockSpec((columns, block), lambda i: (0, i)), shape((columns, rows), bf16))
    else:
        out = (row_blocks(block, columns), far_shape((rows, columns), bf16))
    return call(
        functools.partial(hidden_kernel, sides, want),
        "hidden_" + want,
        [(place, smem)]
        + [(a if want == "value" else far(a), row_blocks(block, width)) for a in table]
        + [far(q_low), far(bias.reshape(1, columns))],
        [out],
        grid=(rows // block,),
        after=after,
    )[0]


def pool_kernel(last, hidden_ref, matrix_ref, *refs):
    for g in range(matrix_ref.shape[0]):
        total = dot(hidden_ref[...], matrix_ref[g], (1, 0))
        nodes = total.shape[1]
        at = slice(g * nodes, (g + 1) * nodes)
        if last:
            refs[1][at, :] = (refs[0][:, at] + total).T.astype(bf16)
        else:
            refs[0][:, at] = total


def pool(hidden_t, matrix, first, so_far, after=()):
    columns, rows = hidden_t.shape
    groups, _, node_dev = matrix.shape
    nodes = groups * node_dev
    last = so_far is not None
    total_block = pl.BlockSpec((columns, 2 * node_dev), lambda i: (0, i))
    return call(
        functools.partial(pool_kernel, last),
        "pool",
        [hidden_t, (matrix, pl.BlockSpec((2, rows, node_dev), lambda i: (i, first // rows, 0)))]
        + ([(so_far, total_block)] if last else []),
        [
            (row_blocks(2 * node_dev, columns), shape((nodes, columns), bf16))
            if last
            else (total_block, shape((columns, nodes), f32))
        ],
        grid=(groups // 2,),
        after=after,
    )[0]


def first_rows(table, nodes):
    return [(far(a), pl.BlockSpec((nodes, a.shape[1]), lambda *_: (0, 0))) for a in table]


def self_kernel(sides, place_ref, *refs):
    own, (w_ref, bias_ref, cotangent_ref), outs = refs[:sides], refs[sides : sides + 3], refs[sides + 3 : -1]
    pre_ref = refs[-1]
    width = own[0].shape[1]
    pre = bias_ref[...]
    for j in range(sides):
        pre = pre + dot(own[j][...], rows_at(w_ref, (place_ref[1] ^ j) * width, width)[...], (1, 0))
    pre_ref[...] = pre
    few, columns = outs[0].shape[0], pre.shape[1]
    for j in range(sides):
        at = (place_ref[1] ^ j) * few
        outs[j][:, 0:columns] = rows_at(pre_ref, at, few)[...]
        outs[j][:, columns:] = rows_at(cotangent_ref, at, few)[...]


def self_half(place, table, w_self, bias, cotangent, after=()):
    nodes, columns = cotangent.shape
    sides = len(table)
    return call(
        functools.partial(self_kernel, sides),
        "self_half",
        [(place, smem)] + first_rows(table, nodes) + [far(w_self), far(bias.reshape(1, columns)), far(cotangent)],
        [full((nodes // sides, 2 * columns), f32, far_shape)] * sides,
        scratch=[pltpu.VMEM((nodes, columns), f32)],
        after=after,
    )


def combine_kernel(node_total, sides, parts_ref, *refs):
    early, w_refs = refs[:sides], refs[sides : 2 * sides]
    grad_ref, pooled_ref, late = refs[2 * sides], refs[2 * sides + 1], refs[2 * sides + 2 :]
    groups, _, few, columns = parts_ref.shape
    pooled = []
    for m in range(sides):
        total = parts_ref[0, m].astype(f32)
        for g in range(1, groups):
            total = total + parts_ref[g, m].astype(f32)
        pooled.append(total.astype(bf16))
    pooled = jnp.concatenate(pooled, axis=1)
    pooled_ref[...] = pooled
    activated, slope, squares, cross = [], [], 0.0, 0.0
    for j in range(sides):
        pre = early[j][:, 0:columns] + dot(pooled, w_refs[j][...], (1, 0))
        a, s = gelu_parts(pre)
        activated.append(a)
        slope.append(s)
        squares = squares + jnp.sum(a * a, axis=1, keepdims=True)
        cross = cross + jnp.sum(a * early[j][:, columns:], axis=1, keepdims=True)
    scale = lax.rsqrt(squares + epsilon)
    pull = cross * scale * scale * scale
    grad_pooled = 0.0
    square_high, square_low = halves(jnp.sum(squares, axis=0, keepdims=True))
    index = lax.broadcasted_iota(i32, (extra_rows, late[0].shape[1]), 0)
    extra = jnp.where(
        index == 0, square_high.astype(f32), jnp.where(index == 1, square_low.astype(f32), 0.0)
    ).astype(bf16)
    for j in range(sides):
        grad_act = early[j][:, columns:] * scale - activated[j] * pull + (2.0 * penalty_rate / node_total) * activated[j]
        grad = (grad_act * slope[j]).astype(bf16)
        grad_pooled = grad_pooled + dot(grad, w_refs[j][...], (1, 1))
        late[j][0:few, 0:columns] = (activated[j] * scale).astype(bf16)
        late[j][0:few, columns:] = grad
        late[j][few:, :] = extra
    for m in range(sides):
        part = grad_pooled[:, m * columns : (m + 1) * columns].astype(bf16)
        for g in range(groups):
            grad_ref[g, m] = part


def combine(node_total, parts, early, w_pooled, after=()):
    groups, sides, few, columns = parts.shape
    return call(
        functools.partial(combine_kernel, node_total, sides),
        "combine",
        [parts, *map(far, early), *map(far, w_pooled)],
        [full(parts.shape, bf16), full((few, sides * columns), bf16, far_shape)]
        + [full((few + extra_rows, 2 * columns), bf16, far_shape)] * sides,
        after=after,
    )


def w_back_kernel(sides, place_ref, *refs):
    own, late, pooled = refs[:sides], refs[sides : 2 * sides], refs[2 * sides : 3 * sides]
    (w_ref, emb_ref, even_ref, odd_ref, extra_ref, *self_refs), scratch = refs[3 * sides : -3], refs[-3:]
    grad_ref, pooled_ref, total_ref = scratch
    nodes, columns = emb_ref.shape
    few = nodes // sides
    squares = 0.0
    for j in range(sides):
        at = (place_ref[1] ^ j) * few
        rows_at(emb_ref, at, few)[...] = late[j][0:few, 0:columns].astype(f32)
        rows_at(grad_ref, at, few)[...] = late[j][0:few, columns:]
        rows_at(pooled_ref, at, few)[...] = pooled[j][...]
        squares = squares + late[j][few : few + 1, 0:columns].astype(f32)
        squares = squares + late[j][few + 1 : few + 2, 0:columns].astype(f32)
    grad = grad_ref[...]
    for j in range(sides):
        side = place_ref[1] ^ j
        rows_at(total_ref, side * columns, columns)[...] = dot(own[j][...], grad, (0, 0))
        self_refs[j][...] = dot(grad, rows_at(w_ref, side * columns, columns)[...], (1, 1)).astype(bf16)
    total_ref[sides * columns :, :] = dot(pooled_ref[...], grad, (0, 0))
    bias_high, bias_low = halves(jnp.sum(grad.astype(f32), axis=0, keepdims=True))
    square_high, square_low = halves(squares)
    index = lax.broadcasted_iota(i32, (extra_rows, columns), 0)
    extra = jnp.zeros(index.shape, f32)
    for i, row in enumerate((bias_high, bias_low, square_high, square_low)):
        extra = jnp.where(index == 2 + i, row.astype(f32), extra)
    extra_ref[...] = extra.astype(bf16)
    count, piece, _ = even_ref.shape
    for s in range(count):
        even_ref[s] = rows_at(total_ref, (place_ref[0] ^ (2 * s)) * piece, piece)[...].astype(bf16)
        odd_ref[s] = rows_at(total_ref, (place_ref[0] ^ (2 * s + 1)) * piece, piece)[...].astype(bf16)


def w_back(place, table, late, pooled, w_self, node_dev, groups, after=()):
    sides = len(table)
    rows, columns = 2 * w_self.shape[0], w_self.shape[1]
    half = full((groups // 2, rows // groups, columns), bf16, far_shape)
    return call(
        functools.partial(w_back_kernel, sides),
        "w_back",
        [(place, smem)] + first_rows(table, node_dev) + [*map(far, late), *map(far, pooled), far(w_self)],
        [full((node_dev, columns), f32, far_shape), half, half]
        + [full((extra_rows, columns), bf16, far_shape)]
        + [full((node_dev, columns), bf16, far_shape)] * sides,
        scratch=[
            pltpu.VMEM((node_dev, columns), bf16),
            pltpu.VMEM((node_dev, sides * columns), bf16),
            pltpu.VMEM((rows, columns), f32),
        ],
        after=after,
    )


def add_pairs_kernel(own_ref, other_ref, *outs):
    for i, out in enumerate(outs):
        out[...] = (own_ref[i].astype(f32) + other_ref[i].astype(f32)).astype(bf16)


def add_pairs(own, other, after=()):
    count, rows, columns = own.shape
    return call(
        add_pairs_kernel, "add_pairs", [far(own), far(other)], [full((rows, columns), bf16, far_shape)] * count, after=after
    )


def add_some_kernel(count, *refs):
    total = refs[0][...].astype(f32)
    for ref in refs[1:count]:
        total = total + ref[...].astype(f32)
    refs[count][...] = total.astype(bf16)


def add_some(parts, after=()):
    return call(
        functools.partial(add_some_kernel, len(parts)), "add_some", parts, [full(parts[0].shape, bf16, far_shape)], after=after
    )[0]


def collect_kernel(count, place_ref, *refs):
    piece = refs[0].shape[0]
    for i in range(count):
        rows_at(refs[count], (place_ref[0] ^ i) * piece, piece)[...] = refs[i][...].astype(f32)


def collect(place, pieces, after=()):
    rows, columns = pieces[0].shape
    return call(
        functools.partial(collect_kernel, len(pieces)),
        "collect",
        [(place, smem), *pieces],
        [full((len(pieces) * rows, columns), f32, far_shape)],
        after=after,
    )[0]


def add_kernel(scale, parts_ref, piece_ref, q_bias_ref, w_bias_ref, scalar_ref):
    groups, rows, _ = parts_ref.shape
    total = parts_ref[0].astype(f32)
    for g in range(1, groups):
        total = total + parts_ref[g].astype(f32)
    piece = rows - extra_rows
    low = total[0:piece, :].astype(bf16)
    for g in range(groups):
        piece_ref[g] = low
    pairs = [total[piece + 2 * i : piece + 2 * i + 1, :] + total[piece + 2 * i + 1 : piece + 2 * i + 2, :] for i in range(3)]
    q_bias_ref[...] = pairs[0]
    w_bias_ref[...] = pairs[1]
    scalar_ref[...] = scale * pairs[2][:, 0:1]


def add(parts, scale, after=()):
    groups, rows, columns = parts.shape
    return call(
        functools.partial(add_kernel, scale),
        "add",
        [parts],
        [full((groups, rows - extra_rows, columns), bf16), full((1, columns), f32), full((1, columns), f32), full((1, 1), f32)],
        after=after,
    )


def widen_kernel(low_ref, out_ref):
    out_ref[...] = low_ref[...].astype(f32)


def widen(low, after=()):
    rows, columns = low.shape
    block = rows // 2
    return call(
        widen_kernel,
        "widen",
        [(low, row_blocks(block, columns))],
        [(row_blocks(block, columns), far_shape((rows, columns), f32))],
        grid=(2,),
        after=after,
    )[0]


def rows_back_kernel(chunk_counts, sides, place_ref, *refs):
    chunks = len(chunk_counts)
    matrix_ref, pooled_ref, slopes = refs[0], refs[1], refs[2 : 2 + chunks]
    table = refs[2 + chunks : 2 + chunks + chunks * sides]
    rest = refs[2 + chunks + chunks * sides :]
    extra_ref, grad_refs, (q_ref, total_ref, bias_ref) = rest[0], rest[1 : 1 + chunks], rest[1 + chunks :]
    step = pl.program_id(0)
    matrix = jnp.concatenate([matrix_ref[g] for g in range(matrix_ref.shape[0])], axis=1)
    summed = dot(matrix, pooled_ref[...], (1, 0))
    width = table[0].shape[1]

    @pl.when(step == 0)
    def _():
        bias_ref[...] = jnp.zeros_like(bias_ref)
        total_ref[...] = jnp.zeros_like(total_ref)

    first = 0
    for k in range(chunks):

        @pl.when((step >= first) & (step < first + chunk_counts[k]))
        def _():
            grad = summed * slopes[k][...].astype(f32)
            bias_ref[...] += jnp.sum(grad, axis=0, keepdims=True)
            grad = grad.astype(bf16)
            grad_refs[k][...] = grad
            for j in range(sides):
                total_ref[j] += dot(grad, table[k * sides + j][...], (0, 0))

        first += chunk_counts[k]

    @pl.when(step == pl.num_programs(0) - 1)
    def _():
        high, low = halves(bias_ref[...])
        groups, rows, columns = q_ref.shape
        index = lax.broadcasted_iota(i32, (extra_rows, columns), 0)
        extra = extra_ref[...].astype(f32)
        extra = jnp.where(index == 0, high.astype(f32), jnp.where(index == 1, low.astype(f32), extra)).astype(bf16)
        piece = rows - extra_rows
        per = width // piece
        for g in range(groups):
            q_ref[g, piece:, :] = extra
        for j in range(sides):
            flat = total_ref[j].T.astype(bf16)
            for part in range(per):
                q_ref[(place_ref[1] ^ j) * per + part, 0:piece, :] = flat[part * piece : (part + 1) * piece, :]


def rows_back(place, matrix, pooled, slopes, table, extra, after=()):
    sides = len(table[0])
    groups, row_dev, node_dev = matrix.shape
    columns, width = pooled.shape[1], table[0][0].shape[1]
    block = min(slopes[-1].shape[0], 512 * 2048 // (groups * node_dev))
    specs = chunk_specs(slopes, block)
    by_side = [chunk_specs([part[j] for part in table], block) for j in range(sides)]
    return call(
        functools.partial(rows_back_kernel, [a.shape[0] // block for a in slopes], sides),
        "rows_back",
        [(place, smem), (far(matrix), pl.BlockSpec((groups, block, node_dev), lambda i: (0, i, 0))), pooled]
        + list(zip(map(far, slopes), specs))
        + [(far(table[k][j]), by_side[j][k]) for k in range(len(table)) for j in range(sides)]
        + [far(extra)],
        [(spec, far_shape(a.shape, bf16)) for spec, a in zip(specs, slopes)]
        + [full((groups, sides * width // groups + extra_rows, columns), bf16)],
        grid=(row_dev // block,),
        scratch=[pltpu.VMEM((sides, columns, width), f32), pltpu.VMEM((1, columns), f32)],
        after=after,
    )


def table_back_kernel(sides, nodes, with_self, place_ref, *refs):
    grads, qs, self_refs, out_ref = refs[:sides], refs[sides : 2 * sides], refs[2 * sides : -1], refs[-1]
    width = out_ref.shape[1]
    total = dot(grads[0][...], qs[0][...], (1, 1))
    for j in range(1, sides):
        total = total + dot(grads[j][...], qs[j][...], (1, 1))
    out_ref[...] = total
    if not with_self:
        return

    @pl.when(pl.program_id(0) == 0)
    def _():
        own = self_refs[0][...].astype(f32)
        for ref in self_refs[1:sides]:
            own = own + ref[...].astype(f32)
        out_ref[0:nodes, :] += own


def table_back(place, grads, qs, grad_self, first, row_dev, so_far=None, after=()):
    sides = len(grads)
    rows, columns = grads[0].shape
    nodes, width = grad_self[0].shape
    block = min(rows, 512)
    operands = [(place, smem)] + [(far(a), row_blocks(block, columns)) for a in grads] + [*map(far, qs), *map(far, grad_self)]
    return call(
        functools.partial(table_back_kernel, sides, nodes, first == 0),
        "table_back",
        operands,
        [(pl.BlockSpec((block, width), lambda i: (first // block + i, 0)), far_shape((row_dev, width), f32))],
        grid=(rows // block,),
        after=after if so_far is None else [so_far, *after],
        aliases={} if so_far is None else {len(operands): 0},
    )[0]


def cut_kernel(sides, place_ref, q_ref, *outs):
    width = outs[0].shape[0]
    for j in range(sides):
        outs[j][...] = rows_at(q_ref, (place_ref[1] ^ j) * width, width)[...]


def cut_rows(place, q_low, sides, after=()):
    rows, columns = q_low.shape
    return call(
        functools.partial(cut_kernel, sides),
        "cut",
        [(place, smem), far(q_low)],
        [full((rows // sides, columns), bf16, far_shape)] * sides,
        after=after,
    )


def all_sides(array):
    across = swap(array, "mp", 2)
    return [array, swap(array, "mp", 1), across, swap(across, "mp", 1)]


def shards(table, q_weight, q_bias, w_weight, w_bias, neighbours, counts, importance, cotangent):
    groups = lax.axis_size("dp")
    sides = lax.axis_size("mp")
    row_dev, width = table.shape
    node_dev, _ = neighbours.shape
    node_total = node_dev * groups
    columns = q_weight.shape[1]
    few = node_dev // sides
    place = jnp.stack([lax.axis_index("dp"), lax.axis_index("mp")]).astype(i32)

    cut = row_dev * 3 // 4
    (low_a,) = low([(table, 0, cut)])
    across_a, beside_a = swap(low_a, "mp", 2), swap(low_a, "mp", 1)
    slots = make_slots(place, neighbours, counts, importance, row_dev, groups, after=[low_a])
    half = sides * width
    low_b, q_low, w_self, w_pooled = low(
        [(table, cut, row_dev - cut), (q_weight, 0, half), (w_weight, 0, half), (w_weight, half, half)], after=[slots]
    )
    slots = exchange(slots, "dp")
    across_b, beside_b = swap(low_b, "mp", 2), swap(low_b, "mp", 1)

    matrix = spread(slots, row_dev, after=[low_b])
    across_a = gate(across_a, [matrix])
    part_a = [low_a, beside_a, across_a, swap(across_a, "mp", 1)]
    hidden_a = hidden(place, part_a, q_low, q_bias, "value")
    so_far = pool(hidden_a, matrix, 0, None)
    w_pooled = all_sides(gate(w_pooled, [hidden_a]))
    across_b = gate(across_b, [hidden_a])
    part_b = [low_b, beside_b, across_b, swap(across_b, "mp", 1)]
    parts = [part_a, part_b]
    hidden_b = hidden(place, part_b, q_low, q_bias, "value", after=[so_far])
    part_sums = pool(hidden_b, matrix, cut, so_far, after=[w_pooled[2]])
    pooled = exchange(part_sums.reshape(groups * sides, few, columns), ("dp", "mp"))

    early = self_half(place, part_a, w_self, w_bias, cotangent, after=[part_sums])
    early = [early[0]] + [swap(early[j], "mp", j) for j in range(1, sides)]
    slope = [hidden(place, part, q_low, q_bias, "slope", after=[early[0]]) for part in parts]

    grad_pooled, pooled, *late = combine(
        node_total, pooled.reshape(groups, sides, few, columns), early, w_pooled, after=slope
    )
    grad_pooled = exchange(grad_pooled.reshape(groups * sides, few, columns), ("dp", "mp")).reshape(node_total, columns)
    late = [late[0]] + [swap(late[j], "mp", j) for j in range(1, sides)]
    embedding, even, odd, extra, *grad_self = w_back(
        place, part_a, late, all_sides(pooled), w_self, node_dev, groups
    )
    q_cut = cut_rows(place, q_low, sides, after=[late[0]])
    q_cut = [q_cut[0]] + [swap(q_cut[j], "mp", j) for j in range(1, sides)]
    grad_self = [grad_self[0]] + [swap(grad_self[j], "mp", j) for j in range(1, sides)]

    grad_a, grad_b, q_parts = rows_back(place, matrix, grad_pooled, slope, parts, extra, after=[q_cut[2]])
    pairs = add_pairs(even, swap(odd, "dp", 1), after=[grad_a])
    count = groups // 2
    pairs = [pairs[0]] + [swap(pairs[s], "dp", 2 * s) for s in range(1, count)]
    grad_a = gate(grad_a, [pairs[0]])
    across_a = swap(grad_a, "mp", 2)
    piece = add_some(pairs)
    pieces = [piece] + [swap(piece, "dp", 2 * s) for s in range(1, count)]
    q_pieces, q_bias_grad, w_bias_grad, penalty = add(
        exchange(q_parts, "dp"), penalty_rate / node_total, after=[piece]
    )
    pieces = [p for own in pieces for p in (own, swap(own, "dp", 1))]
    grads = [grad_a, swap(grad_a, "mp", 1), across_a, swap(across_a, "mp", 1)]
    table_grad = table_back(place, grads, q_cut, grad_self, 0, row_dev, after=[pieces[2], pieces[4], pieces[6]])
    across_b = swap(grad_b, "mp", 2)
    grads = [grad_b, swap(grad_b, "mp", 1), across_b, swap(across_b, "mp", 1)]
    table_grad = table_back(place, grads, q_cut, grad_self, grad_a.shape[0], row_dev, table_grad)
    q_grad = widen(exchange(q_pieces, "dp").reshape(-1, columns), after=[table_grad])
    w_grad = collect(place, pieces, after=[table_grad])
    return (
        embedding,
        table_grad,
        q_grad,
        q_bias_grad.reshape(columns),
        w_grad,
        w_bias_grad.reshape(columns),
        penalty.reshape(()),
    )


def solution(mesh):
    placed = (
        P("dp", "mp"),
        P(None, "mp"),
        P("mp"),
        P(None, "mp"),
        P("mp"),
        P("dp", None),
        P("dp"),
        P("dp", None),
        P("dp", "mp"),
    )
    return jax.shard_map(
        shards,
        mesh=mesh,
        in_specs=placed,
        out_specs=(
            P("dp", "mp"),
            P("dp", "mp"),
            P(None, "mp"),
            P("mp"),
            P(None, "mp"),
            P("mp"),
            P(),
        ),
        check_vma=False,
    )
```

```python
import collections
import functools

import jax
import jax.numpy as jnp
from jax import lax
from jax.experimental import pallas as pl
from jax.experimental.pallas import tpu as pltpu
from jax.sharding import PartitionSpec as P

epsilon = 1e-06
penalty_rate = 0.01
bf16, f32, i32, i16 = jnp.bfloat16, jnp.float32, jnp.int32, jnp.int16
bucket_rows = 256
lane_tile = 128
weight_unit = 32767.0
code_step = 64
extra_rows = 16
mib = 1024 * 1024
step_rows = 1024
expected_us = collections.defaultdict(
    lambda: 0.001,
    hidden_slope=5,
    self_half=3,
    combine=4,
    w_back=4,
    rows_back=16,
    add=20,
    add_some=1,
    add_pairs=2,
    table_back=20,
    cut=1,
    collect=2,
    widen=1,
)


def dot(a, b, contract):
    return lax.dot_general(a, b, ((contract[:1], contract[1:]), ((), ())), preferred_element_type=f32)


def gelu_parts(values):
    c = 0.7978845608028654
    squared = values * values
    t = jnp.tanh(c * values * (1.0 + 0.044715 * squared))
    half = 0.5 * (1.0 + t)
    slope = half + 0.5 * values * (1.0 - t * t) * (c * (1.0 + 3 * 0.044715 * squared))
    return values * half, slope


def size(dims, dtype):
    rows = dims[-2] if len(dims) > 1 else 1
    rest = 1
    for d in dims[:-2]:
        rest *= d
    return rest * (-(-rows // 16) * 16) * (-(-dims[-1] // 128) * 128) * jnp.dtype(dtype).itemsize


def far(array):
    return pltpu.with_memory_space_constraint(array, pltpu.HBM)


def far_shape(dims, dtype):
    return pltpu.HBM(dims, dtype)


def call(kernel, name, operands, outs, grid=(1,), scratch=(), after=(), near=(), aliases={}, spare=8):
    after = (*map(far, after), *near)
    specs, arrays, need = [], [], 0
    for operand in operands:
        array, spec = operand if isinstance(operand, tuple) else (operand, whole(operand))
        specs.append(spec)
        arrays.append(array)
        if spec is not smem:
            need += (2 if isinstance(operand, tuple) else 1) * size(spec.block_shape, array.dtype)
    for spec, out in outs:
        need += 2 * size(spec.block_shape, out.dtype)
    for item in scratch:
        need += size(item.shape, item.dtype)
    count = len(arrays)
    inner = lambda *refs: kernel(*refs[:count], *refs[count + len(after) :])
    return pl.pallas_call(
        inner,
        grid=grid,
        in_specs=specs + [pl.BlockSpec(memory_space=pl.ANY)] * len(after),
        out_specs=[o[0] for o in outs],
        out_shape=[o[1] for o in outs],
        scratch_shapes=list(scratch),
        input_output_aliases=dict(aliases),
        compiler_params=pltpu.CompilerParams(vmem_limit_bytes=need + spare * mib),
        cost_estimate=pl.CostEstimate(
            flops=int(expected_us[name] * 1.15e9), bytes_accessed=int(expected_us[name] * 3.69e6), transcendentals=0
        ),
        name=name,
    )(*arrays, *after)


def full(dims, dtype, kind=jax.ShapeDtypeStruct):
    return whole(shape(dims, dtype)), kind(dims, dtype)


def shape(dims, dtype):
    return jax.ShapeDtypeStruct(dims, dtype)


def whole(array):
    return pl.BlockSpec(array.shape, lambda *_: (0,) * array.ndim)


smem = pl.BlockSpec(memory_space=pltpu.SMEM)


def swap(array, axis, bits):
    size = lax.axis_size(axis)
    return lax.ppermute(array, axis, [(i, i ^ bits) for i in range(size)])


def halves(values):
    high = values.astype(bf16)
    return high, (values - high.astype(f32)).astype(bf16)


def exchange(array, axes):
    return lax.all_to_all(array, axes, split_axis=0, concat_axis=0, tiled=True)


def rows_at(ref, start, size):
    return ref.at[pl.ds(pl.multiple_of(start, size), size)]


def row_blocks(block, columns):
    return pl.BlockSpec((block, columns), lambda i: (i, 0))


def chunk_spec(block, columns, first, count):
    return pl.BlockSpec((block, columns), lambda i: (jnp.clip(i - first, 0, count - 1), 0))


def chunk_specs(chunks, block):
    specs, first = [], 0
    for a in chunks:
        count = a.shape[0] // block
        specs.append(chunk_spec(block, a.shape[1], first, count))
        first += count
    return specs


def low_kernel(count, *refs):
    for i in range(count):
        refs[count + i][...] = refs[i][...].astype(bf16)


def low(pieces, steps, after=(), near=()):
    operands, outs = [], []
    for array, first, rows in pieces:
        block, columns = rows // steps, array.shape[1]
        operands.append(
            (far(array), pl.BlockSpec((block, columns), functools.partial(lambda f, i: (f + i, 0), first // block)))
        )
        outs.append((row_blocks(block, columns), far_shape((rows, columns), bf16)))
    return call(functools.partial(low_kernel, len(pieces)), "low", operands, outs, grid=(steps,), after=after, near=near)


def gate_kernel(*refs):
    del refs


def gate(array, after):
    return pl.pallas_call(
        gate_kernel,
        in_specs=[pl.BlockSpec(memory_space=pl.ANY)] * (1 + len(after)),
        out_specs=pl.BlockSpec(memory_space=pl.ANY),
        out_shape=shape(array.shape, array.dtype),
        input_output_aliases={0: 0},
        compiler_params=pltpu.CompilerParams(vmem_limit_bytes=mib),
        cost_estimate=pl.CostEstimate(flops=1, bytes_accessed=1, transcendentals=0),
        name="gate",
    )(array, *after)


def slots_kernel(row_dev, place_ref, ids_ref, counts_ref, importance_ref, out_ref):
    del place_ref
    ids = ids_ref[...]
    index = lax.broadcasted_iota(i32, ids.shape, 0)
    raw = jnp.where(index < counts_ref[...], importance_ref[...], 0.0)
    weight = raw / jnp.sum(raw, axis=0, keepdims=True)
    bucket = jnp.where(weight > 0.0, ids // bucket_rows, -1)
    within = ids - (ids // bucket_rows) * bucket_rows
    merged = jnp.zeros_like(weight)
    rank = jnp.zeros_like(bucket)
    for k in range(ids.shape[0]):
        merged = merged + jnp.where(ids == ids[k : k + 1, :], weight[k : k + 1, :], 0.0)
        rank = rank + jnp.where((bucket == bucket[k : k + 1, :]) & (index > k), 1, 0)
    amount = jnp.round(merged * weight_unit).astype(i32)
    per = row_dev // bucket_rows
    for d in range(out_ref.shape[0]):
        mine = (bucket >= d * per) & (bucket < (d + 1) * per)
        out_ref[d, 0] = jnp.where(mine, (bucket - d * per) * code_step + rank, -1).astype(i16)
        out_ref[d, 1] = within.astype(i16)
        out_ref[d, 2] = amount.astype(i16)


def make_slots(place, neighbours, counts, importance, row_dev, groups, after=()):
    node_dev, slots_node = neighbours.shape
    return call(
        functools.partial(slots_kernel, row_dev),
        "slots",
        [(place, smem), far(neighbours.T), far(counts.reshape(1, node_dev)), far(importance.T)],
        [full((groups, 3, slots_node, node_dev), i16)],
        after=after,
    )[0]


def spread_kernel(slots_ref, out_ref, all_ref, row_ref, amount_ref):
    _, _, slots_node, lanes = slots_ref.shape
    buckets = out_ref.shape[1] // bucket_rows
    tiles = lanes // lane_tile
    codes = slots_ref[0, 0].astype(i32)
    depth = jnp.max(jnp.where(codes >= 0, (codes & (code_step - 1)) + 1, 0).astype(f32)).astype(i32)
    for t in range(tiles):
        at = slice(t * lane_tile, (t + 1) * lane_tile)
        all_ref[t, 0] = codes[:, at].astype(f32)
        all_ref[t, 1] = slots_ref[0, 1, :, at].astype(i32).astype(f32)
        all_ref[t, 2] = slots_ref[0, 2, :, at].astype(i32).astype(f32) * (1.0 / weight_unit)
    eight = lax.broadcasted_iota(i32, (8, lane_tile), 0).astype(f32)

    def extract(t, first):
        target = eight + first
        for start in range(0, buckets, 8):
            some = range(start, min(start + 8, buckets))
            rows = [jnp.full((8, lane_tile), -1.0, f32) for _ in some]
            amounts = [jnp.zeros((8, lane_tile), f32) for _ in some]
            for k in range(slots_node):
                code = jnp.broadcast_to(all_ref[t, 0, k : k + 1, :], (8, lane_tile))
                row = jnp.broadcast_to(all_ref[t, 1, k : k + 1, :], (8, lane_tile))
                amount = jnp.broadcast_to(all_ref[t, 2, k : k + 1, :], (8, lane_tile))
                for i, b in enumerate(some):
                    hit = code == target + float(b * code_step)
                    rows[i] = jnp.where(hit, row, rows[i])
                    amounts[i] = jnp.where(hit, amount, amounts[i])
            for i, b in enumerate(some):
                row_ref[t, b] = rows[i]
                amount_ref[t, b] = amounts[i]

    tall = (bucket_rows // 16, 16, lane_tile)
    row_index = (lax.broadcasted_iota(i32, tall, 0) * 16 + lax.broadcasted_iota(i32, tall, 1)).astype(f32).astype(bf16)

    def place_all(count, add):
        def one(b, carry):
            at = pl.ds(pl.multiple_of(b * bucket_rows, bucket_rows), bucket_rows)
            for t in range(tiles):
                lane = slice(t * lane_tile, (t + 1) * lane_tile)
                total = out_ref[0, at, lane].reshape(tall) if add else jnp.zeros(tall, bf16)
                for j in range(count):
                    row = jnp.broadcast_to(row_ref[t, b, j : j + 1, :], tall[1:]).astype(bf16)
                    amount = jnp.broadcast_to(amount_ref[t, b, j : j + 1, :], tall[1:]).astype(bf16)
                    total = jnp.where(row_index == row[None], amount[None], total)
                out_ref[0, at, lane] = total.reshape(bucket_rows, lane_tile)
            return carry

        lax.fori_loop(0, buckets, one, 0)

    for t in range(tiles):
        extract(t, 0.0)
    for low, high in ((0, 3), (4, 4), (5, 5), (6, 6), (7, slots_node)):

        @pl.when((depth >= low) & (depth <= high))
        def _():
            place_all(min(high, 8), False)

    def more(p, carry):
        for t in range(tiles):
            extract(t, (p * 8).astype(f32))
        place_all(8, True)
        return carry

    lax.fori_loop(1, (depth + 7) // 8, more, 0)


def spread(slots, row_dev, near=()):
    groups, _, slots_node, node_dev = slots.shape
    tiles = node_dev // lane_tile
    buckets = row_dev // bucket_rows
    return call(
        spread_kernel,
        "spread",
        [(slots, pl.BlockSpec((1, 3, slots_node, node_dev), lambda i: (i, 0, 0, 0)))],
        [(pl.BlockSpec((1, row_dev, node_dev), lambda i: (i, 0, 0)), shape((groups, row_dev, node_dev), bf16))],
        grid=(groups,),
        scratch=[
            pltpu.VMEM((tiles, 3, slots_node, lane_tile), f32),
            pltpu.VMEM((tiles, buckets, 8, lane_tile), f32),
            pltpu.VMEM((tiles, buckets, 8, lane_tile), f32),
        ],
        near=near,
    )[0]


def hidden_kernel(sides, want, place_ref, *refs):
    table, q_ref, bias_ref, outs = refs[:sides], refs[sides], refs[sides + 1], refs[sides + 2 :]
    width = table[0].shape[1]
    pre = bias_ref[...]
    for j in range(sides):
        pre = pre + dot(table[j][...], rows_at(q_ref, (place_ref[1] ^ j) * width, width)[...], (1, 0))
    value, slope = gelu_parts(pre)
    if want == "value":
        outs[0][...] = value.astype(bf16).T
    else:
        outs[0][...] = slope.astype(bf16)


def hidden(place, table, q_low, bias, want, after=(), near=()):
    rows, width = table[0].shape
    columns = q_low.shape[1]
    sides = len(table)
    block = min(rows, 512)
    if want == "value":
        out = (pl.BlockSpec((columns, block), lambda i: (0, i)), shape((columns, rows), bf16))
    else:
        out = (row_blocks(block, columns), far_shape((rows, columns), bf16))
    return call(
        functools.partial(hidden_kernel, sides, want),
        "hidden_" + want,
        [(place, smem)]
        + [(a if want == "value" else far(a), row_blocks(block, width)) for a in table]
        + [far(q_low), far(bias.reshape(1, columns))],
        [out],
        grid=(rows // block,),
        after=after,
        near=near,
    )[0]


def pool_kernel(last, views, hidden_ref, *refs):
    matrix, refs = refs[:views], refs[views:]
    rows = matrix[0].shape[1]
    for g in range(matrix[0].shape[0]):
        total = dot(hidden_ref[:, 0:rows], matrix[0][g], (1, 0))
        for v in range(1, views):
            total = total + dot(hidden_ref[:, v * rows : (v + 1) * rows], matrix[v][g], (1, 0))
        nodes = total.shape[1]
        at = slice(g * nodes, (g + 1) * nodes)
        if len(refs) > 1:
            total = total + refs[0][:, at]
        if last:
            refs[-1][at, :] = total.T.astype(bf16)
        else:
            refs[-1][:, at] = total


def pool(hidden_t, matrix, first, so_far, step_rows, last, near=()):
    columns, rows = hidden_t.shape
    groups, _, node_dev = matrix.shape
    nodes = groups * node_dev
    views = rows // step_rows
    total_block = pl.BlockSpec((columns, 2 * node_dev), lambda i: (0, i))
    block = (2, step_rows, node_dev)
    view = [pl.BlockSpec(block, functools.partial(lambda v, i: (i, v, 0), first // step_rows + v)) for v in range(views)]
    return call(
        functools.partial(pool_kernel, last, views),
        "pool",
        [hidden_t] + [(matrix, spec) for spec in view] + ([] if so_far is None else [(so_far, total_block)]),
        [
            (row_blocks(2 * node_dev, columns), shape((nodes, columns), bf16))
            if last
            else (total_block, shape((columns, nodes), f32))
        ],
        grid=(groups // 2,),
        near=near,
    )[0]


def first_rows(table, nodes):
    return [(far(a), pl.BlockSpec((nodes, a.shape[1]), lambda *_: (0, 0))) for a in table]


def self_kernel(sides, place_ref, *refs):
    own, (w_ref, bias_ref, cotangent_ref), outs = refs[:sides], refs[sides : sides + 3], refs[sides + 3 : -1]
    pre_ref = refs[-1]
    width = own[0].shape[1]
    pre = bias_ref[...]
    for j in range(sides):
        pre = pre + dot(own[j][...], rows_at(w_ref, (place_ref[1] ^ j) * width, width)[...], (1, 0))
    pre_ref[...] = pre
    few, columns = outs[0].shape[0], pre.shape[1]
    for j in range(sides):
        at = (place_ref[1] ^ j) * few
        outs[j][:, 0:columns] = rows_at(pre_ref, at, few)[...]
        outs[j][:, columns:] = rows_at(cotangent_ref, at, few)[...]


def self_half(place, table, w_self, bias, cotangent, near=()):
    nodes, columns = cotangent.shape
    sides = len(table)
    return call(
        functools.partial(self_kernel, sides),
        "self_half",
        [(place, smem)] + first_rows(table, nodes) + [far(w_self), far(bias.reshape(1, columns)), far(cotangent)],
        [full((nodes // sides, 2 * columns), f32, far_shape)] * sides,
        scratch=[pltpu.VMEM((nodes, columns), f32)],
        near=near,
    )


def combine_kernel(node_total, sides, parts_ref, *refs):
    early, w_refs = refs[:sides], refs[sides : 2 * sides]
    grad_ref, pooled_ref, late = refs[2 * sides], refs[2 * sides + 1], refs[2 * sides + 2 :]
    groups, _, few, columns = parts_ref.shape
    pooled = []
    for m in range(sides):
        total = parts_ref[0, m].astype(f32)
        for g in range(1, groups):
            total = total + parts_ref[g, m].astype(f32)
        pooled.append(total.astype(bf16))
    pooled = jnp.concatenate(pooled, axis=1)
    pooled_ref[...] = pooled
    activated, slope, squares, cross = [], [], 0.0, 0.0
    for j in range(sides):
        pre = early[j][:, 0:columns] + dot(pooled, w_refs[j][...], (1, 0))
        a, s = gelu_parts(pre)
        activated.append(a)
        slope.append(s)
        squares = squares + jnp.sum(a * a, axis=1, keepdims=True)
        cross = cross + jnp.sum(a * early[j][:, columns:], axis=1, keepdims=True)
    scale = lax.rsqrt(squares + epsilon)
    pull = cross * scale * scale * scale
    grad_pooled = 0.0
    square_high, square_low = halves(jnp.sum(squares, axis=0, keepdims=True))
    index = lax.broadcasted_iota(i32, (extra_rows, late[0].shape[1]), 0)
    extra = jnp.where(
        index == 0, square_high.astype(f32), jnp.where(index == 1, square_low.astype(f32), 0.0)
    ).astype(bf16)
    for j in range(sides):
        grad_act = early[j][:, columns:] * scale - activated[j] * pull + (2.0 * penalty_rate / node_total) * activated[j]
        grad = (grad_act * slope[j]).astype(bf16)
        grad_pooled = grad_pooled + dot(grad, w_refs[j][...], (1, 1))
        late[j][0:few, 0:columns] = (activated[j] * scale).astype(bf16)
        late[j][0:few, columns:] = grad
        late[j][few:, :] = extra
    for m in range(sides):
        part = grad_pooled[:, m * columns : (m + 1) * columns].astype(bf16)
        for g in range(groups):
            grad_ref[g, m] = part


def combine(node_total, parts, early, w_pooled, after=()):
    groups, sides, few, columns = parts.shape
    return call(
        functools.partial(combine_kernel, node_total, sides),
        "combine",
        [parts, *map(far, early), *map(far, w_pooled)],
        [full(parts.shape, bf16), full((few, sides * columns), bf16, far_shape)]
        + [full((few + extra_rows, 2 * columns), bf16, far_shape)] * sides,
        after=after,
    )


def w_back_kernel(sides, place_ref, *refs):
    own, late, pooled = refs[:sides], refs[sides : 2 * sides], refs[2 * sides : 3 * sides]
    (w_ref, emb_ref, even_ref, odd_ref, extra_ref, *self_refs), scratch = refs[3 * sides : -3], refs[-3:]
    grad_ref, pooled_ref, total_ref = scratch
    nodes, columns = emb_ref.shape
    few = nodes // sides
    squares = 0.0
    for j in range(sides):
        at = (place_ref[1] ^ j) * few
        rows_at(emb_ref, at, few)[...] = late[j][0:few, 0:columns].astype(f32)
        rows_at(grad_ref, at, few)[...] = late[j][0:few, columns:]
        rows_at(pooled_ref, at, few)[...] = pooled[j][...]
        squares = squares + late[j][few : few + 1, 0:columns].astype(f32)
        squares = squares + late[j][few + 1 : few + 2, 0:columns].astype(f32)
    grad = grad_ref[...]
    for j in range(sides):
        side = place_ref[1] ^ j
        rows_at(total_ref, side * columns, columns)[...] = dot(own[j][...], grad, (0, 0))
        self_refs[j][...] = dot(grad, rows_at(w_ref, side * columns, columns)[...], (1, 1)).astype(bf16)
    total_ref[sides * columns :, :] = dot(pooled_ref[...], grad, (0, 0))
    bias_high, bias_low = halves(jnp.sum(grad.astype(f32), axis=0, keepdims=True))
    square_high, square_low = halves(squares)
    index = lax.broadcasted_iota(i32, (extra_rows, columns), 0)
    extra = jnp.zeros(index.shape, f32)
    for i, row in enumerate((bias_high, bias_low, square_high, square_low)):
        extra = jnp.where(index == 2 + i, row.astype(f32), extra)
    extra_ref[...] = extra.astype(bf16)
    count, piece, _ = even_ref.shape
    for s in range(count):
        even_ref[s] = rows_at(total_ref, (place_ref[0] ^ (2 * s)) * piece, piece)[...].astype(bf16)
        odd_ref[s] = rows_at(total_ref, (place_ref[0] ^ (2 * s + 1)) * piece, piece)[...].astype(bf16)


def w_back(place, table, late, pooled, w_self, node_dev, groups, after=()):
    sides = len(table)
    rows, columns = 2 * w_self.shape[0], w_self.shape[1]
    half = full((groups // 2, rows // groups, columns), bf16, far_shape)
    return call(
        functools.partial(w_back_kernel, sides),
        "w_back",
        [(place, smem)] + first_rows(table, node_dev) + [*late, *pooled, far(w_self)],
        [full((node_dev, columns), f32, far_shape), half, half]
        + [full((extra_rows, columns), bf16, far_shape)]
        + [full((node_dev, columns), bf16, far_shape)] * sides,
        scratch=[
            pltpu.VMEM((node_dev, columns), bf16),
            pltpu.VMEM((node_dev, sides * columns), bf16),
            pltpu.VMEM((rows, columns), f32),
        ],
        after=after,
    )


def add_pairs_kernel(own_ref, other_ref, *outs):
    for i, out in enumerate(outs):
        out[...] = (own_ref[i].astype(f32) + other_ref[i].astype(f32)).astype(bf16)


def add_pairs(own, other, after=(), near=()):
    count, rows, columns = own.shape
    return call(
        add_pairs_kernel, "add_pairs", [far(own), other], [full((rows, columns), bf16, far_shape)] * count, after=after, near=near
    )


def add_some_kernel(count, *refs):
    total = refs[0][...].astype(f32)
    for ref in refs[1:count]:
        total = total + ref[...].astype(f32)
    refs[count][...] = total.astype(bf16)


def add_some(parts, after=()):
    return call(
        functools.partial(add_some_kernel, len(parts)), "add_some", parts, [full(parts[0].shape, bf16, far_shape)], after=after
    )[0]


def collect_kernel(count, place_ref, *refs):
    piece = refs[0].shape[0]
    for i in range(count):
        rows_at(refs[count], (place_ref[0] ^ i) * piece, piece)[...] = refs[i][...].astype(f32)


def collect(place, pieces, after=()):
    rows, columns = pieces[0].shape
    return call(
        functools.partial(collect_kernel, len(pieces)),
        "collect",
        [(place, smem), *pieces],
        [full((len(pieces) * rows, columns), f32, far_shape)],
        after=after,
    )[0]


def add_kernel(scale, parts_ref, piece_ref, q_bias_ref, w_bias_ref, scalar_ref):
    groups, rows, _ = parts_ref.shape
    total = parts_ref[0].astype(f32)
    for g in range(1, groups):
        total = total + parts_ref[g].astype(f32)
    piece = rows - extra_rows
    low = total[0:piece, :].astype(bf16)
    for g in range(groups):
        piece_ref[g] = low
    pairs = [total[piece + 2 * i : piece + 2 * i + 1, :] + total[piece + 2 * i + 1 : piece + 2 * i + 2, :] for i in range(3)]
    q_bias_ref[...] = pairs[0]
    w_bias_ref[...] = pairs[1]
    scalar_ref[...] = scale * pairs[2][:, 0:1]


def add(parts, scale, after=()):
    groups, rows, columns = parts.shape
    return call(
        functools.partial(add_kernel, scale),
        "add",
        [parts],
        [full((groups, rows - extra_rows, columns), bf16), full((1, columns), f32), full((1, columns), f32), full((1, 1), f32)],
        after=after,
    )


def widen_kernel(low_ref, out_ref):
    out_ref[...] = low_ref[...].astype(f32)


def widen(low, after=()):
    rows, columns = low.shape
    block = rows // 2
    return call(
        widen_kernel,
        "widen",
        [(low, row_blocks(block, columns))],
        [(row_blocks(block, columns), far_shape((rows, columns), f32))],
        grid=(2,),
        after=after,
    )[0]


def each_chunk(step, counts, run):
    first = 0
    for k, count in enumerate(counts):
        pl.when((step >= first) & (step < first + count))(functools.partial(run, k))
        first += count


def rows_back_kernel(chunk_counts, grad_counts, sides, place_ref, *refs):
    chunks = len(chunk_counts)
    matrix_ref, pooled_ref, slopes = refs[0], refs[1], refs[2 : 2 + chunks]
    table = refs[2 + chunks : 2 + chunks + chunks * sides]
    extra_ref, rest = refs[2 + chunks + chunks * sides], refs[3 + chunks + chunks * sides :]
    grad_refs, (q_ref, total_ref, bias_ref, low_ref) = rest[: len(grad_counts)], rest[len(grad_counts) :]
    step = pl.program_id(0)
    matrix = jnp.concatenate([matrix_ref[g] for g in range(matrix_ref.shape[0])], axis=1)
    summed = dot(matrix, pooled_ref[...], (1, 0))
    width = table[0].shape[1]

    @pl.when(step == 0)
    def _():
        bias_ref[...] = jnp.zeros_like(bias_ref)
        total_ref[...] = jnp.zeros_like(total_ref)

    def in_chunk(k):
        grad = summed * slopes[k][...].astype(f32)
        bias_ref[...] += jnp.sum(grad, axis=0, keepdims=True)
        grad = grad.astype(bf16)
        low_ref[...] = grad
        for j in range(sides):
            total_ref[j] += dot(grad, table[k * sides + j][...], (0, 0))

    def put(k):
        grad_refs[k][...] = low_ref[...]

    each_chunk(step, chunk_counts, in_chunk)
    each_chunk(step, grad_counts, put)

    @pl.when(step == pl.num_programs(0) - 1)
    def _():
        high, low = halves(bias_ref[...])
        groups, rows, columns = q_ref.shape
        index = lax.broadcasted_iota(i32, (extra_rows, columns), 0)
        extra = extra_ref[...].astype(f32)
        extra = jnp.where(index == 0, high.astype(f32), jnp.where(index == 1, low.astype(f32), extra)).astype(bf16)
        piece = rows - extra_rows
        per = width // piece
        for g in range(groups):
            q_ref[g, piece:, :] = extra
        for j in range(sides):
            flat = total_ref[j].T.astype(bf16)
            for part in range(per):
                q_ref[(place_ref[1] ^ j) * per + part, 0:piece, :] = flat[part * piece : (part + 1) * piece, :]


def rows_back(place, matrix, pooled, slopes, table, extra, grad_rows, near=()):
    sides = len(table[0])
    groups, row_dev, node_dev = matrix.shape
    columns, width = pooled.shape[1], table[0][0].shape[1]
    block = min(min(a.shape[0] for a in slopes), step_rows * 2048 // (groups * node_dev))
    by_side = [chunk_specs([part[j] for part in table], block) for j in range(sides)]
    grads = [shape((rows, columns), bf16) for rows in grad_rows]
    return call(
        functools.partial(rows_back_kernel, [a.shape[0] // block for a in slopes], [r // block for r in grad_rows], sides),
        "rows_back",
        [(place, smem), (far(matrix), pl.BlockSpec((groups, block, node_dev), lambda i: (0, i, 0))), pooled]
        + list(zip(map(far, slopes), chunk_specs(slopes, block)))
        + [(far(table[k][j]), by_side[j][k]) for k in range(len(table)) for j in range(sides)]
        + [far(extra)],
        [(spec, far_shape(a.shape, bf16)) for spec, a in zip(chunk_specs(grads, block), grads)]
        + [full((groups, sides * width // groups + extra_rows, columns), bf16)],
        grid=(row_dev // block,),
        scratch=[
            pltpu.VMEM((sides, columns, width), f32),
            pltpu.VMEM((1, columns), f32),
            pltpu.VMEM((block, columns), bf16),
        ],
        near=near,
    )


def table_back_kernel(sides, nodes, with_self, place_ref, *refs):
    grads, qs, self_refs, out_ref = refs[:sides], refs[sides : 2 * sides], refs[2 * sides : -1], refs[-1]
    width = out_ref.shape[1]
    total = dot(grads[0][...], qs[0][...], (1, 1))
    for j in range(1, sides):
        total = total + dot(grads[j][...], qs[j][...], (1, 1))
    out_ref[...] = total
    if not with_self:
        return

    @pl.when(pl.program_id(0) == 0)
    def _():
        own = self_refs[0][...].astype(f32)
        for ref in self_refs[1:sides]:
            own = own + ref[...].astype(f32)
        out_ref[0:nodes, :] += own


def table_back(place, grads, qs, grad_self, first, row_dev, so_far=None, near=()):
    sides = len(grads)
    rows, columns = grads[0].shape
    nodes, width = grad_self[0].shape
    block = min(rows, 512)
    operands = [(place, smem)] + [(far(a), row_blocks(block, columns)) for a in grads] + [*map(far, qs), *map(far, grad_self)]
    return call(
        functools.partial(table_back_kernel, sides, nodes, first == 0),
        "table_back",
        operands,
        [(pl.BlockSpec((block, width), lambda i: (first // block + i, 0)), far_shape((row_dev, width), f32))],
        grid=(rows // block,),
        after=() if so_far is None else [so_far],
        near=near,
        aliases={} if so_far is None else {len(operands): 0},
    )[0]


def cut_kernel(sides, place_ref, q_ref, *outs):
    width = outs[0].shape[0]
    for j in range(sides):
        outs[j][...] = rows_at(q_ref, (place_ref[1] ^ j) * width, width)[...]


def cut_rows(place, q_low, sides, after=()):
    rows, columns = q_low.shape
    return call(
        functools.partial(cut_kernel, sides),
        "cut",
        [(place, smem), far(q_low)],
        [full((rows // sides, columns), bf16, far_shape)] * sides,
        after=after,
    )


def all_sides(array):
    across = swap(array, "mp", 2)
    return [array, swap(array, "mp", 1), across, swap(across, "mp", 1)]


def shards(table, q_weight, q_bias, w_weight, w_bias, neighbours, counts, importance, cotangent):
    groups = lax.axis_size("dp")
    sides = lax.axis_size("mp")
    row_dev, width = table.shape
    node_dev, _ = neighbours.shape
    node_total = node_dev * groups
    columns = q_weight.shape[1]
    few = node_dev // sides
    place = jnp.stack([lax.axis_index("dp"), lax.axis_index("mp")]).astype(i32)

    unit = row_dev // 4
    (low_a,) = low([(table, 0, unit)], 1)
    low_b, low_c = low([(table, unit, 2 * unit), (table, 3 * unit, unit)], 2, after=[low_a])
    across_a, beside_a = swap(low_a, "mp", 2), swap(low_a, "mp", 1)
    slots = make_slots(place, neighbours, counts, importance, row_dev, groups, after=[low_b])
    half = sides * width
    q_low, w_self, w_pooled = low([(q_weight, 0, half), (w_weight, 0, half), (w_weight, half, half)], 4, near=[slots])
    low_b = gate(low_b, [across_a])
    across_b, beside_b = swap(low_b, "mp", 2), swap(low_b, "mp", 1)
    slots = exchange(slots, "dp")

    part_a = [low_a, beside_a, across_a, swap(across_a, "mp", 1)]
    hidden_a = hidden(place, part_a, q_low, q_bias, "value")
    matrix = spread(slots, row_dev, near=[hidden_a])
    so_far = pool(hidden_a, matrix, 0, None, unit, False)
    low_c = gate(low_c, [across_b])
    across_c, beside_c = swap(low_c, "mp", 2), swap(low_c, "mp", 1)
    across_b = gate(across_b, [matrix])
    part_b = [low_b, beside_b, across_b, swap(across_b, "mp", 1)]
    hidden_b = hidden(place, part_b, q_low, q_bias, "value", near=[so_far])
    so_far = pool(hidden_b, matrix, unit, so_far, unit, False)
    across_c = gate(across_c, [hidden_b])
    part_c = [low_c, beside_c, across_c, swap(across_c, "mp", 1)]
    parts = [part_a, part_b, part_c]
    hidden_c = hidden(place, part_c, q_low, q_bias, "value", near=[so_far])
    w_pooled = all_sides(gate(w_pooled, [matrix]))
    part_sums = pool(hidden_c, matrix, 3 * unit, so_far, unit, True)
    pooled = exchange(part_sums.reshape(groups * sides, few, columns), ("dp", "mp"))

    early = self_half(place, part_a, w_self, w_bias, cotangent, near=[part_sums, w_pooled[2]])
    early = [early[0]] + [swap(early[j], "mp", j) for j in range(1, sides)]
    slope = [hidden(place, part, q_low, q_bias, "slope", after=[early[0]]) for part in parts]

    grad_pooled, pooled, *late = combine(
        node_total, pooled.reshape(groups, sides, few, columns), early, w_pooled, after=slope
    )
    grad_pooled = exchange(grad_pooled.reshape(groups * sides, few, columns), ("dp", "mp")).reshape(node_total, columns)
    late = [late[0]] + [swap(late[j], "mp", j) for j in range(1, sides)]
    embedding, even, odd, extra, *grad_self = w_back(
        place, part_a, late, all_sides(pooled), w_self, node_dev, groups
    )
    q_cut = cut_rows(place, q_low, sides, after=[late[0]])
    q_cut = [q_cut[0]] + [swap(q_cut[j], "mp", j) for j in range(1, sides)]
    grad_self = [grad_self[0]] + [swap(grad_self[j], "mp", j) for j in range(1, sides)]

    grad_a, grad_b, q_parts = rows_back(place, matrix, grad_pooled, slope, parts, extra, [unit, 3 * unit], near=[q_cut[2]])
    pairs = add_pairs(even, swap(odd, "dp", 1), after=[grad_a], near=[grad_self[2], grad_self[3]])
    count = groups // 2
    pairs = [pairs[0]] + [swap(pairs[s], "dp", 2 * s) for s in range(1, count)]
    grad_b = gate(grad_b, [pairs[0]])
    across_b = swap(grad_b, "mp", 2)
    piece = add_some(pairs)
    pieces = [piece] + [swap(piece, "dp", 2 * s) for s in range(1, count)]
    q_pieces, q_bias_grad, w_bias_grad, penalty = add(
        exchange(q_parts, "dp"), penalty_rate / node_total, after=[piece]
    )
    pieces = [p for own in pieces for p in (own, swap(own, "dp", 1))]
    grads = [grad_b, swap(grad_b, "mp", 1), across_b, swap(across_b, "mp", 1)]
    table_grad = table_back(place, grads, q_cut, grad_self, unit, row_dev, near=[pieces[2], pieces[4], pieces[6]])
    across_a = swap(grad_a, "mp", 2)
    grads = [grad_a, swap(grad_a, "mp", 1), across_a, swap(across_a, "mp", 1)]
    table_grad = table_back(place, grads, q_cut, grad_self, 0, row_dev, table_grad)
    q_grad = widen(exchange(q_pieces, "dp").reshape(-1, columns), after=[table_grad])
    w_grad = collect(place, pieces, after=[table_grad])
    return (
        embedding,
        table_grad,
        q_grad,
        q_bias_grad.reshape(columns),
        w_grad,
        w_bias_grad.reshape(columns),
        penalty.reshape(()),
    )


def solution(mesh):
    placed = (
        P("dp", "mp"),
        P(None, "mp"),
        P("mp"),
        P(None, "mp"),
        P("mp"),
        P("dp", None),
        P("dp"),
        P("dp", None),
        P("dp", "mp"),
    )
    return jax.shard_map(
        shards,
        mesh=mesh,
        in_specs=placed,
        out_specs=(
            P("dp", "mp"),
            P("dp", "mp"),
            P(None, "mp"),
            P("mp"),
            P(None, "mp"),
            P("mp"),
            P(),
        ),
        check_vma=False,
    )
```

```python
import collections
import functools

import jax
import jax.numpy as jnp
from jax import lax
from jax.experimental import pallas as pl
from jax.experimental.pallas import tpu as pltpu
from jax.sharding import PartitionSpec as P

epsilon = 1e-06
penalty_rate = 0.01
bf16, f32, i32, i16 = jnp.bfloat16, jnp.float32, jnp.int32, jnp.int16
bucket_rows = 256
lane_tile = 128
weight_unit = 32767.0
code_step = 64
extra_rows = 16
mib = 1024 * 1024
step_rows = 1024
expected_us = collections.defaultdict(
    lambda: 0.001,
    hidden_slope=5,
    self_half=3,
    combine=1,
    w_back=4,
    rows_back=16,
    add=20,
    add_some=1,
    add_pairs=2,
    table_back=20,
    cut=1,
    collect=2,
    widen=1,
)


def dot(a, b, contract):
    return lax.dot_general(a, b, ((contract[:1], contract[1:]), ((), ())), preferred_element_type=f32)


def gelu_parts(values):
    c = 0.7978845608028654
    squared = values * values
    t = jnp.tanh(c * values * (1.0 + 0.044715 * squared))
    half = 0.5 * (1.0 + t)
    slope = half + 0.5 * values * (1.0 - t * t) * (c * (1.0 + 3 * 0.044715 * squared))
    return values * half, slope


def size(dims, dtype):
    rows = dims[-2] if len(dims) > 1 else 1
    rest = 1
    for d in dims[:-2]:
        rest *= d
    return rest * (-(-rows // 16) * 16) * (-(-dims[-1] // 128) * 128) * jnp.dtype(dtype).itemsize


def far(array):
    return pltpu.with_memory_space_constraint(array, pltpu.HBM)


def far_shape(dims, dtype):
    return pltpu.HBM(dims, dtype)


def call(kernel, name, operands, outs, grid=(1,), scratch=(), after=(), near=(), aliases={}, spare=8):
    after = (*map(far, after), *near)
    specs, arrays, need = [], [], 0
    for operand in operands:
        array, spec = operand if isinstance(operand, tuple) else (operand, whole(operand))
        specs.append(spec)
        arrays.append(array)
        if spec is not smem:
            need += (2 if isinstance(operand, tuple) else 1) * size(spec.block_shape, array.dtype)
    for spec, out in outs:
        need += 2 * size(spec.block_shape, out.dtype)
    for item in scratch:
        need += size(item.shape, item.dtype)
    count = len(arrays)
    inner = lambda *refs: kernel(*refs[:count], *refs[count + len(after) :])
    return pl.pallas_call(
        inner,
        grid=grid,
        in_specs=specs + [pl.BlockSpec(memory_space=pl.ANY)] * len(after),
        out_specs=[o[0] for o in outs],
        out_shape=[o[1] for o in outs],
        scratch_shapes=list(scratch),
        input_output_aliases=dict(aliases),
        compiler_params=pltpu.CompilerParams(vmem_limit_bytes=need + spare * mib),
        cost_estimate=pl.CostEstimate(
            flops=int(expected_us[name] * 1.15e9), bytes_accessed=int(expected_us[name] * 3.69e6), transcendentals=0
        ),
        name=name,
    )(*arrays, *after)


def full(dims, dtype, kind=jax.ShapeDtypeStruct):
    return whole(shape(dims, dtype)), kind(dims, dtype)


def shape(dims, dtype):
    return jax.ShapeDtypeStruct(dims, dtype)


def whole(array):
    return pl.BlockSpec(array.shape, lambda *_: (0,) * array.ndim)


smem = pl.BlockSpec(memory_space=pltpu.SMEM)


def swap(array, axis, bits):
    size = lax.axis_size(axis)
    return lax.ppermute(array, axis, [(i, i ^ bits) for i in range(size)])


def halves(values):
    high = values.astype(bf16)
    return high, (values - high.astype(f32)).astype(bf16)


def exchange(array, axes):
    return lax.all_to_all(array, axes, split_axis=0, concat_axis=0, tiled=True)


def rows_at(ref, start, size):
    return ref.at[pl.ds(pl.multiple_of(start, size), size)]


def row_blocks(block, columns):
    return pl.BlockSpec((block, columns), lambda i: (i, 0))


def each_chunk(step, counts, run):
    first = 0
    for k, count in enumerate(counts):
        pl.when((step >= first) & (step < first + count))(functools.partial(run, k))
        first += count


def chunk_spec(block, columns, first, count):
    return pl.BlockSpec((block, columns), lambda i: (jnp.clip(i - first, 0, count - 1), 0))


def chunk_specs(chunks, block):
    specs, first = [], 0
    for a in chunks:
        count = a.shape[0] // block
        specs.append(chunk_spec(block, a.shape[1], first, count))
        first += count
    return specs


def low_kernel(count, *refs):
    for i in range(count):
        refs[count + i][...] = refs[i][...].astype(bf16)


def low(pieces, steps, after=(), near=()):
    operands, outs = [], []
    for array, first, rows in pieces:
        block, columns = rows // steps, array.shape[1]
        operands.append(
            (far(array), pl.BlockSpec((block, columns), functools.partial(lambda f, i: (f + i, 0), first // block)))
        )
        outs.append((row_blocks(block, columns), far_shape((rows, columns), bf16)))
    return call(functools.partial(low_kernel, len(pieces)), "low", operands, outs, grid=(steps,), after=after, near=near)


def gate_kernel(*refs):
    del refs


def gate(array, after):
    return pl.pallas_call(
        gate_kernel,
        in_specs=[pl.BlockSpec(memory_space=pl.ANY)] * (1 + len(after)),
        out_specs=pl.BlockSpec(memory_space=pl.ANY),
        out_shape=shape(array.shape, array.dtype),
        input_output_aliases={0: 0},
        compiler_params=pltpu.CompilerParams(vmem_limit_bytes=mib),
        cost_estimate=pl.CostEstimate(flops=1, bytes_accessed=1, transcendentals=0),
        name="gate",
    )(array, *after)


def slots_kernel(row_dev, place_ref, ids_ref, counts_ref, importance_ref, out_ref):
    del place_ref
    ids = ids_ref[...]
    index = lax.broadcasted_iota(i32, ids.shape, 0)
    raw = jnp.where(index < counts_ref[...], importance_ref[...], 0.0)
    weight = raw / jnp.sum(raw, axis=0, keepdims=True)
    bucket = jnp.where(weight > 0.0, ids // bucket_rows, -1)
    within = ids - (ids // bucket_rows) * bucket_rows
    merged = jnp.zeros_like(weight)
    rank = jnp.zeros_like(bucket)
    for k in range(ids.shape[0]):
        merged = merged + jnp.where(ids == ids[k : k + 1, :], weight[k : k + 1, :], 0.0)
        rank = rank + jnp.where((bucket == bucket[k : k + 1, :]) & (index > k), 1, 0)
    amount = jnp.round(merged * weight_unit).astype(i32)
    per = row_dev // bucket_rows
    for d in range(out_ref.shape[0]):
        mine = (bucket >= d * per) & (bucket < (d + 1) * per)
        out_ref[d, 0] = jnp.where(mine, (bucket - d * per) * code_step + rank, -1).astype(i16)
        out_ref[d, 1] = within.astype(i16)
        out_ref[d, 2] = amount.astype(i16)


def make_slots(place, neighbours, counts, importance, row_dev, groups, after=()):
    node_dev, slots_node = neighbours.shape
    return call(
        functools.partial(slots_kernel, row_dev),
        "slots",
        [(place, smem), far(neighbours.T), far(counts.reshape(1, node_dev)), far(importance.T)],
        [full((groups, 3, slots_node, node_dev), i16)],
        after=after,
    )[0]


def spread_kernel(slots_ref, out_ref, all_ref, row_ref, amount_ref):
    _, _, slots_node, lanes = slots_ref.shape
    buckets = out_ref.shape[1] // bucket_rows
    tiles = lanes // lane_tile
    codes = slots_ref[0, 0].astype(i32)
    depth = jnp.max(jnp.where(codes >= 0, (codes & (code_step - 1)) + 1, 0).astype(f32)).astype(i32)
    for t in range(tiles):
        at = slice(t * lane_tile, (t + 1) * lane_tile)
        all_ref[t, 0] = codes[:, at].astype(f32)
        all_ref[t, 1] = slots_ref[0, 1, :, at].astype(i32).astype(f32)
        all_ref[t, 2] = slots_ref[0, 2, :, at].astype(i32).astype(f32) * (1.0 / weight_unit)
    eight = lax.broadcasted_iota(i32, (8, lane_tile), 0).astype(f32)

    def extract(t, first):
        target = eight + first
        for start in range(0, buckets, 8):
            some = range(start, min(start + 8, buckets))
            rows = [jnp.full((8, lane_tile), -1.0, f32) for _ in some]
            amounts = [jnp.zeros((8, lane_tile), f32) for _ in some]
            for k in range(slots_node):
                code = jnp.broadcast_to(all_ref[t, 0, k : k + 1, :], (8, lane_tile))
                row = jnp.broadcast_to(all_ref[t, 1, k : k + 1, :], (8, lane_tile))
                amount = jnp.broadcast_to(all_ref[t, 2, k : k + 1, :], (8, lane_tile))
                for i, b in enumerate(some):
                    hit = code == target + float(b * code_step)
                    rows[i] = jnp.where(hit, row, rows[i])
                    amounts[i] = jnp.where(hit, amount, amounts[i])
            for i, b in enumerate(some):
                row_ref[t, b] = rows[i]
                amount_ref[t, b] = amounts[i]

    tall = (bucket_rows // 16, 16, lane_tile)
    row_index = (lax.broadcasted_iota(i32, tall, 0) * 16 + lax.broadcasted_iota(i32, tall, 1)).astype(f32).astype(bf16)

    def place_all(count, add):
        def one(b, carry):
            at = pl.ds(pl.multiple_of(b * bucket_rows, bucket_rows), bucket_rows)
            for t in range(tiles):
                lane = slice(t * lane_tile, (t + 1) * lane_tile)
                total = out_ref[0, at, lane].reshape(tall) if add else jnp.zeros(tall, bf16)
                for j in range(count):
                    row = jnp.broadcast_to(row_ref[t, b, j : j + 1, :], tall[1:]).astype(bf16)
                    amount = jnp.broadcast_to(amount_ref[t, b, j : j + 1, :], tall[1:]).astype(bf16)
                    total = jnp.where(row_index == row[None], amount[None], total)
                out_ref[0, at, lane] = total.reshape(bucket_rows, lane_tile)
            return carry

        lax.fori_loop(0, buckets, one, 0)

    for t in range(tiles):
        extract(t, 0.0)
    for low, high in ((0, 3), (4, 4), (5, 5), (6, 6), (7, slots_node)):

        @pl.when((depth >= low) & (depth <= high))
        def _():
            place_all(min(high, 8), False)

    def more(p, carry):
        for t in range(tiles):
            extract(t, (p * 8).astype(f32))
        place_all(8, True)
        return carry

    lax.fori_loop(1, (depth + 7) // 8, more, 0)


def spread(slots, first, count, row_dev, near=()):
    _, _, slots_node, node_dev = slots.shape
    tiles = node_dev // lane_tile
    buckets = row_dev // bucket_rows
    return call(
        spread_kernel,
        "spread",
        [(slots, pl.BlockSpec((1, 3, slots_node, node_dev), lambda i: (first + i, 0, 0, 0)))],
        [(pl.BlockSpec((1, row_dev, node_dev), lambda i: (i, 0, 0)), shape((count, row_dev, node_dev), bf16))],
        grid=(count,),
        scratch=[
            pltpu.VMEM((tiles, 3, slots_node, lane_tile), f32),
            pltpu.VMEM((tiles, buckets, 8, lane_tile), f32),
            pltpu.VMEM((tiles, buckets, 8, lane_tile), f32),
        ],
        near=near,
    )[0]


def hidden_kernel(sides, want, place_ref, *refs):
    table, q_ref, bias_ref, outs = refs[:sides], refs[sides], refs[sides + 1], refs[sides + 2 :]
    width = table[0].shape[1]
    pre = bias_ref[...]
    for j in range(sides):
        pre = pre + dot(table[j][...], rows_at(q_ref, (place_ref[1] ^ j) * width, width)[...], (1, 0))
    value, slope = gelu_parts(pre)
    if want == "value":
        outs[0][...] = value.astype(bf16).T
    else:
        outs[0][...] = slope.astype(bf16)


def hidden(place, table, q_low, bias, want, after=(), near=()):
    rows, width = table[0].shape
    columns = q_low.shape[1]
    sides = len(table)
    block = min(rows, 512)
    if want == "value":
        out = (pl.BlockSpec((columns, block), lambda i: (0, i)), shape((columns, rows), bf16))
    else:
        out = (row_blocks(block, columns), far_shape((rows, columns), bf16))
    return call(
        functools.partial(hidden_kernel, sides, want),
        "hidden_" + want,
        [(place, smem)]
        + [(a if want == "value" else far(a), row_blocks(block, width)) for a in table]
        + [far(q_low), far(bias.reshape(1, columns))],
        [out],
        grid=(rows // block,),
        after=after,
        near=near,
    )[0]


def pool_kernel(last, parts, counts, *refs):
    hidden_refs, refs = refs[: len(counts)], refs[len(counts) :]
    views = sum(counts)
    matrix, refs = refs[: parts * views], refs[parts * views :]
    groups, rows, nodes = matrix[0].shape
    steps = pl.num_programs(0) // parts

    def one_part(p):
        for g in range(groups):
            total, v = None, p * views
            for hidden_ref, count in zip(hidden_refs, counts):
                for k in range(count):
                    term = dot(hidden_ref[:, k * rows : (k + 1) * rows], matrix[v][g], (1, 0))
                    total, v = term if total is None else total + term, v + 1
            at = slice(g * nodes, (g + 1) * nodes)
            if len(refs) > 1:
                total = total + refs[0][:, at]
            if last:
                refs[-1][at, :] = total.T.astype(bf16)
            else:
                refs[-1][:, at] = total

    each_chunk(pl.program_id(0), [steps] * parts, one_part)


def pool(hidden_t, matrix, first, so_far, step_rows, last, near=()):
    columns = hidden_t[0].shape[0]
    per, _, node_dev = matrix[0].shape
    parts, counts = len(matrix), [a.shape[1] // step_rows for a in hidden_t]
    nodes = parts * per * node_dev
    steps = per // 2
    total_block = pl.BlockSpec((columns, 2 * node_dev), lambda i: (0, i))
    operands = list(hidden_t)
    for p in range(parts):
        for v in range(sum(counts)):
            index = functools.partial(lambda p, v, i: (jnp.clip(i - p * steps, 0, steps - 1), v, 0), p, first // step_rows + v)
            operands.append((matrix[p], pl.BlockSpec((2, step_rows, node_dev), index)))
    return call(
        functools.partial(pool_kernel, last, parts, counts),
        "pool",
        operands + ([] if so_far is None else [(so_far, total_block)]),
        [
            (row_blocks(2 * node_dev, columns), shape((nodes, columns), bf16))
            if last
            else (total_block, shape((columns, nodes), f32))
        ],
        grid=(parts * steps,),
        near=near,
    )[0]


def first_rows(table, nodes):
    return [(far(a), pl.BlockSpec((nodes, a.shape[1]), lambda *_: (0, 0))) for a in table]


def self_kernel(sides, place_ref, *refs):
    own, (w_ref, bias_ref, cotangent_ref), outs = refs[:sides], refs[sides : sides + 3], refs[sides + 3 : -1]
    pre_ref = refs[-1]
    width = own[0].shape[1]
    pre = bias_ref[...]
    for j in range(sides):
        pre = pre + dot(own[j][...], rows_at(w_ref, (place_ref[1] ^ j) * width, width)[...], (1, 0))
    pre_ref[...] = pre
    few, columns = outs[0].shape[0], pre.shape[1]
    for j in range(sides):
        at = (place_ref[1] ^ j) * few
        outs[j][:, 0:columns] = rows_at(pre_ref, at, few)[...]
        outs[j][:, columns:] = rows_at(cotangent_ref, at, few)[...]


def self_half(place, table, w_self, bias, cotangent, near=()):
    nodes, columns = cotangent.shape
    sides = len(table)
    return call(
        functools.partial(self_kernel, sides),
        "self_half",
        [(place, smem)] + first_rows(table, nodes) + [far(w_self), far(bias.reshape(1, columns)), far(cotangent)],
        [full((nodes // sides, 2 * columns), f32, far_shape)] * sides,
        scratch=[pltpu.VMEM((nodes, columns), f32)],
        near=near,
    )


def combine_kernel(node_total, sides, parts_ref, *refs):
    early, w_refs = refs[:sides], refs[sides : 2 * sides]
    grad_ref, pooled_ref, late = refs[2 * sides], refs[2 * sides + 1], refs[2 * sides + 2 :]
    groups, _, few, columns = parts_ref.shape
    pooled = []
    for m in range(sides):
        total = parts_ref[0, m].astype(f32)
        for g in range(1, groups):
            total = total + parts_ref[g, m].astype(f32)
        pooled.append(total.astype(bf16))
    pooled = jnp.concatenate(pooled, axis=1)
    pooled_ref[...] = pooled
    activated, slope, squares, cross = [], [], 0.0, 0.0
    for j in range(sides):
        pre = early[j][:, 0:columns] + dot(pooled, w_refs[j][...], (1, 0))
        a, s = gelu_parts(pre)
        activated.append(a)
        slope.append(s)
        squares = squares + jnp.sum(a * a, axis=1, keepdims=True)
        cross = cross + jnp.sum(a * early[j][:, columns:], axis=1, keepdims=True)
    scale = lax.rsqrt(squares + epsilon)
    pull = cross * scale * scale * scale
    grad_pooled = 0.0
    square_high, square_low = halves(jnp.sum(squares, axis=0, keepdims=True))
    index = lax.broadcasted_iota(i32, (extra_rows, late[0].shape[1]), 0)
    extra = jnp.where(
        index == 0, square_high.astype(f32), jnp.where(index == 1, square_low.astype(f32), 0.0)
    ).astype(bf16)
    for j in range(sides):
        grad_act = early[j][:, columns:] * scale - activated[j] * pull + (2.0 * penalty_rate / node_total) * activated[j]
        grad = (grad_act * slope[j]).astype(bf16)
        grad_pooled = grad_pooled + dot(grad, w_refs[j][...], (1, 1))
        late[j][0:few, 0:columns] = (activated[j] * scale).astype(bf16)
        late[j][0:few, columns:] = grad
        late[j][few:, :] = extra
    for m in range(sides):
        part = grad_pooled[:, m * columns : (m + 1) * columns].astype(bf16)
        for g in range(groups):
            grad_ref[g, m] = part


def combine(node_total, parts, early, w_pooled, after=()):
    groups, sides, few, columns = parts.shape
    return call(
        functools.partial(combine_kernel, node_total, sides),
        "combine",
        [parts, *map(far, early), *map(far, w_pooled)],
        [full(parts.shape, bf16), full((few, sides * columns), bf16, far_shape)]
        + [full((few + extra_rows, 2 * columns), bf16, far_shape)] * sides,
        after=after,
    )


def w_back_kernel(sides, place_ref, *refs):
    own, late, pooled = refs[:sides], refs[sides : 2 * sides], refs[2 * sides : 3 * sides]
    (w_ref, emb_ref, even_ref, odd_ref, extra_ref, *self_refs), scratch = refs[3 * sides : -3], refs[-3:]
    grad_ref, pooled_ref, total_ref = scratch
    nodes, columns = emb_ref.shape
    few = nodes // sides
    squares = 0.0
    for j in range(sides):
        at = (place_ref[1] ^ j) * few
        rows_at(emb_ref, at, few)[...] = late[j][0:few, 0:columns].astype(f32)
        rows_at(grad_ref, at, few)[...] = late[j][0:few, columns:]
        rows_at(pooled_ref, at, few)[...] = pooled[j][...]
        squares = squares + late[j][few : few + 1, 0:columns].astype(f32)
        squares = squares + late[j][few + 1 : few + 2, 0:columns].astype(f32)
    grad = grad_ref[...]
    for j in range(sides):
        side = place_ref[1] ^ j
        rows_at(total_ref, side * columns, columns)[...] = dot(own[j][...], grad, (0, 0))
        self_refs[j][...] = dot(grad, rows_at(w_ref, side * columns, columns)[...], (1, 1)).astype(bf16)
    total_ref[sides * columns :, :] = dot(pooled_ref[...], grad, (0, 0))
    bias_high, bias_low = halves(jnp.sum(grad.astype(f32), axis=0, keepdims=True))
    square_high, square_low = halves(squares)
    index = lax.broadcasted_iota(i32, (extra_rows, columns), 0)
    extra = jnp.zeros(index.shape, f32)
    for i, row in enumerate((bias_high, bias_low, square_high, square_low)):
        extra = jnp.where(index == 2 + i, row.astype(f32), extra)
    extra_ref[...] = extra.astype(bf16)
    count, piece, _ = even_ref.shape
    for s in range(count):
        even_ref[s] = rows_at(total_ref, (place_ref[0] ^ (2 * s)) * piece, piece)[...].astype(bf16)
        odd_ref[s] = rows_at(total_ref, (place_ref[0] ^ (2 * s + 1)) * piece, piece)[...].astype(bf16)


def w_back(place, table, late, pooled, w_self, node_dev, groups, after=()):
    sides = len(table)
    rows, columns = 2 * w_self.shape[0], w_self.shape[1]
    half = full((groups // 2, rows // groups, columns), bf16, far_shape)
    return call(
        functools.partial(w_back_kernel, sides),
        "w_back",
        [(place, smem)] + first_rows(table, node_dev) + [*late, *pooled, far(w_self)],
        [full((node_dev, columns), f32, far_shape), half, half]
        + [full((extra_rows, columns), bf16, far_shape)]
        + [full((node_dev, columns), bf16, far_shape)] * sides,
        scratch=[
            pltpu.VMEM((node_dev, columns), bf16),
            pltpu.VMEM((node_dev, sides * columns), bf16),
            pltpu.VMEM((rows, columns), f32),
        ],
        after=after,
    )


def add_pairs_kernel(own_ref, other_ref, *outs):
    for i, out in enumerate(outs):
        out[...] = (own_ref[i].astype(f32) + other_ref[i].astype(f32)).astype(bf16)


def add_pairs(own, other, after=(), near=()):
    count, rows, columns = own.shape
    return call(
        add_pairs_kernel, "add_pairs", [far(own), other], [full((rows, columns), bf16, far_shape)] * count, after=after, near=near
    )


def add_some_kernel(count, *refs):
    total = refs[0][...].astype(f32)
    for ref in refs[1:count]:
        total = total + ref[...].astype(f32)
    refs[count][...] = total.astype(bf16)


def add_some(parts, after=()):
    return call(
        functools.partial(add_some_kernel, len(parts)), "add_some", parts, [full(parts[0].shape, bf16, far_shape)], after=after
    )[0]


def collect_kernel(count, place_ref, *refs):
    piece = refs[0].shape[0]
    for i in range(count):
        rows_at(refs[count], (place_ref[0] ^ i) * piece, piece)[...] = refs[i][...].astype(f32)


def collect(place, pieces, after=()):
    rows, columns = pieces[0].shape
    return call(
        functools.partial(collect_kernel, len(pieces)),
        "collect",
        [(place, smem), *pieces],
        [full((len(pieces) * rows, columns), f32, far_shape)],
        after=after,
    )[0]


def add_kernel(scale, parts_ref, piece_ref, q_bias_ref, w_bias_ref, scalar_ref):
    groups, rows, _ = parts_ref.shape
    total = parts_ref[0].astype(f32)
    for g in range(1, groups):
        total = total + parts_ref[g].astype(f32)
    piece = rows - extra_rows
    low = total[0:piece, :].astype(bf16)
    for g in range(groups):
        piece_ref[g] = low
    pairs = [total[piece + 2 * i : piece + 2 * i + 1, :] + total[piece + 2 * i + 1 : piece + 2 * i + 2, :] for i in range(3)]
    q_bias_ref[...] = pairs[0]
    w_bias_ref[...] = pairs[1]
    scalar_ref[...] = scale * pairs[2][:, 0:1]


def add(parts, scale, after=()):
    groups, rows, columns = parts.shape
    return call(
        functools.partial(add_kernel, scale),
        "add",
        [parts],
        [full((groups, rows - extra_rows, columns), bf16), full((1, columns), f32), full((1, columns), f32), full((1, 1), f32)],
        after=after,
    )


def widen_kernel(low_ref, out_ref):
    out_ref[...] = low_ref[...].astype(f32)


def widen(low, after=()):
    rows, columns = low.shape
    block = rows // 2
    return call(
        widen_kernel,
        "widen",
        [(low, row_blocks(block, columns))],
        [(row_blocks(block, columns), far_shape((rows, columns), f32))],
        grid=(2,),
        after=after,
    )[0]


def rows_back_kernel(chunk_counts, grad_counts, sides, parts, place_ref, *refs):
    chunks = len(chunk_counts)
    matrix, refs = refs[:parts], refs[parts:]
    pooled_ref, slopes, table = refs[0], refs[1 : 1 + chunks], refs[1 + chunks : 1 + chunks + chunks * sides]
    extra_ref, rest = refs[1 + chunks + chunks * sides], refs[2 + chunks + chunks * sides :]
    grad_refs, (q_ref, total_ref, bias_ref, low_ref) = rest[: len(grad_counts)], rest[len(grad_counts) :]
    step = pl.program_id(0)
    matrix = jnp.concatenate([part[g] for part in matrix for g in range(part.shape[0])], axis=1)
    summed = dot(matrix, pooled_ref[...], (1, 0))
    width = table[0].shape[1]

    @pl.when(step == 0)
    def _():
        bias_ref[...] = jnp.zeros_like(bias_ref)
        total_ref[...] = jnp.zeros_like(total_ref)

    def in_chunk(k):
        grad = summed * slopes[k][...].astype(f32)
        bias_ref[...] += jnp.sum(grad, axis=0, keepdims=True)
        grad = grad.astype(bf16)
        low_ref[...] = grad
        for j in range(sides):
            total_ref[j] += dot(grad, table[k * sides + j][...], (0, 0))

    def put(k):
        grad_refs[k][...] = low_ref[...]

    each_chunk(step, chunk_counts, in_chunk)
    each_chunk(step, grad_counts, put)

    @pl.when(step == pl.num_programs(0) - 1)
    def _():
        high, low = halves(bias_ref[...])
        groups, rows, columns = q_ref.shape
        index = lax.broadcasted_iota(i32, (extra_rows, columns), 0)
        extra = extra_ref[...].astype(f32)
        extra = jnp.where(index == 0, high.astype(f32), jnp.where(index == 1, low.astype(f32), extra)).astype(bf16)
        piece = rows - extra_rows
        per = width // piece
        for g in range(groups):
            q_ref[g, piece:, :] = extra
        for j in range(sides):
            flat = total_ref[j].T.astype(bf16)
            for part in range(per):
                q_ref[(place_ref[1] ^ j) * per + part, 0:piece, :] = flat[part * piece : (part + 1) * piece, :]


def rows_back(place, matrix, pooled, slopes, table, extra, grad_rows, near=()):
    sides = len(table[0])
    per, row_dev, node_dev = matrix[0].shape
    groups = per * len(matrix)
    columns, width = pooled.shape[1], table[0][0].shape[1]
    block = min(min(a.shape[0] for a in slopes), step_rows * 2048 // (groups * node_dev))
    by_side = [chunk_specs([part[j] for part in table], block) for j in range(sides)]
    grads = [shape((rows, columns), bf16) for rows in grad_rows]
    return call(
        functools.partial(rows_back_kernel, [a.shape[0] // block for a in slopes], [r // block for r in grad_rows], sides, len(matrix)),
        "rows_back",
        [(place, smem)]
        + [(far(part), pl.BlockSpec((per, block, node_dev), lambda i: (0, i, 0))) for part in matrix]
        + [pooled]
        + list(zip(map(far, slopes), chunk_specs(slopes, block)))
        + [(far(table[k][j]), by_side[j][k]) for k in range(len(table)) for j in range(sides)]
        + [far(extra)],
        [(spec, far_shape(a.shape, bf16)) for spec, a in zip(chunk_specs(grads, block), grads)]
        + [full((groups, sides * width // groups + extra_rows, columns), bf16)],
        grid=(row_dev // block,),
        scratch=[
            pltpu.VMEM((sides, columns, width), f32),
            pltpu.VMEM((1, columns), f32),
            pltpu.VMEM((block, columns), bf16),
        ],
        near=near,
    )


def table_back_kernel(sides, nodes, with_self, place_ref, *refs):
    grads, qs, self_refs, out_ref = refs[:sides], refs[sides : 2 * sides], refs[2 * sides : -1], refs[-1]
    width = out_ref.shape[1]
    total = dot(grads[0][...], qs[0][...], (1, 1))
    for j in range(1, sides):
        total = total + dot(grads[j][...], qs[j][...], (1, 1))
    out_ref[...] = total
    if not with_self:
        return

    @pl.when(pl.program_id(0) == 0)
    def _():
        own = self_refs[0][...].astype(f32)
        for ref in self_refs[1:sides]:
            own = own + ref[...].astype(f32)
        out_ref[0:nodes, :] += own


def table_back(place, grads, qs, grad_self, first, row_dev, so_far=None, near=()):
    sides = len(grads)
    rows, columns = grads[0].shape
    nodes, width = grad_self[0].shape
    block = min(rows, 512)
    operands = [(place, smem)] + [(far(a), row_blocks(block, columns)) for a in grads] + [*map(far, qs), *map(far, grad_self)]
    return call(
        functools.partial(table_back_kernel, sides, nodes, first == 0),
        "table_back",
        operands,
        [(pl.BlockSpec((block, width), lambda i: (first // block + i, 0)), far_shape((row_dev, width), f32))],
        grid=(rows // block,),
        after=() if so_far is None else [so_far],
        near=near,
        aliases={} if so_far is None else {len(operands): 0},
    )[0]


def cut_kernel(sides, place_ref, q_ref, *outs):
    width = outs[0].shape[0]
    for j in range(sides):
        outs[j][...] = rows_at(q_ref, (place_ref[1] ^ j) * width, width)[...]


def cut_rows(place, q_low, sides, after=()):
    rows, columns = q_low.shape
    return call(
        functools.partial(cut_kernel, sides),
        "cut",
        [(place, smem), far(q_low)],
        [full((rows // sides, columns), bf16, far_shape)] * sides,
        after=after,
    )


def all_sides(array):
    across = swap(array, "mp", 2)
    return [array, swap(array, "mp", 1), across, swap(across, "mp", 1)]


def shards(table, q_weight, q_bias, w_weight, w_bias, neighbours, counts, importance, cotangent):
    groups = lax.axis_size("dp")
    sides = lax.axis_size("mp")
    row_dev, width = table.shape
    node_dev, _ = neighbours.shape
    node_total = node_dev * groups
    columns = q_weight.shape[1]
    few = node_dev // sides
    place = jnp.stack([lax.axis_index("dp"), lax.axis_index("mp")]).astype(i32)

    unit = row_dev // 4
    (low_a,) = low([(table, 0, unit)], 1)
    low_b, low_c = low([(table, unit, 2 * unit), (table, 3 * unit, unit)], 2, after=[low_a])
    across_a, beside_a = swap(low_a, "mp", 2), swap(low_a, "mp", 1)
    slots = make_slots(place, neighbours, counts, importance, row_dev, groups, after=[low_b])
    half = sides * width
    q_low, w_self, w_pooled = low([(q_weight, 0, half), (w_weight, 0, half), (w_weight, half, half)], 4, near=[slots])
    low_b = gate(low_b, [across_a])
    across_b, beside_b = swap(low_b, "mp", 2), swap(low_b, "mp", 1)
    slots = exchange(slots, "dp")

    part_a = [low_a, beside_a, across_a, swap(across_a, "mp", 1)]
    hidden_a = hidden(place, part_a, q_low, q_bias, "value")
    first = spread(slots, 0, groups // 2, row_dev, near=[hidden_a])
    across_b = gate(across_b, [first])
    low_c = gate(low_c, [across_b])
    across_c, beside_c = swap(low_c, "mp", 2), swap(low_c, "mp", 1)
    matrix = [first, spread(slots, groups // 2, groups // 2, row_dev)]
    part_b = [low_b, beside_b, across_b, swap(across_b, "mp", 1)]
    hidden_b = hidden(place, part_b, q_low, q_bias, "value", near=[matrix[1]])
    so_far = pool([hidden_a, hidden_b], matrix, 0, None, unit, False)
    across_c = gate(across_c, [hidden_b])
    part_c = [low_c, beside_c, across_c, swap(across_c, "mp", 1)]
    parts = [part_a, part_b, part_c]
    hidden_c = hidden(place, part_c, q_low, q_bias, "value", near=[so_far])
    w_pooled = all_sides(gate(w_pooled, [matrix[1]]))
    part_sums = pool([hidden_c], matrix, 3 * unit, so_far, unit, True)
    pooled = exchange(part_sums.reshape(groups * sides, few, columns), ("dp", "mp"))

    early = self_half(place, part_a, w_self, w_bias, cotangent, near=[part_sums, w_pooled[2]])
    early = [early[0]] + [swap(early[j], "mp", j) for j in range(1, sides)]
    slope = [hidden(place, part, q_low, q_bias, "slope", after=[early[0]]) for part in parts]

    grad_pooled, pooled, *late = combine(
        node_total, pooled.reshape(groups, sides, few, columns), early, w_pooled, after=slope
    )
    grad_pooled = exchange(grad_pooled.reshape(groups * sides, few, columns), ("dp", "mp")).reshape(node_total, columns)
    late = [late[0]] + [swap(late[j], "mp", j) for j in range(1, sides)]
    embedding, even, odd, extra, *grad_self = w_back(
        place, part_a, late, all_sides(pooled), w_self, node_dev, groups
    )
    q_cut = cut_rows(place, q_low, sides, after=[slope[0]])
    q_cut = [q_cut[0]] + [swap(q_cut[j], "mp", j) for j in range(1, sides)]
    grad_self = [grad_self[0]] + [swap(grad_self[j], "mp", j) for j in range(1, sides)]

    grad_a, grad_b, q_parts = rows_back(place, matrix, grad_pooled, slope, parts, extra, [unit, 3 * unit], near=[q_cut[2]])
    pairs = add_pairs(even, swap(odd, "dp", 1), after=[grad_a], near=[grad_self[1], grad_self[2], grad_self[3]])
    count = groups // 2
    pairs = [pairs[0]] + [swap(pairs[s], "dp", 2 * s) for s in range(1, count)]
    grad_b = gate(grad_b, [pairs[0]])
    across_b = swap(grad_b, "mp", 2)
    piece = add_some(pairs)
    pieces = [piece] + [swap(piece, "dp", 2 * s) for s in range(1, count)]
    q_pieces, q_bias_grad, w_bias_grad, penalty = add(
        exchange(q_parts, "dp"), penalty_rate / node_total, after=[piece]
    )
    pieces = [p for own in pieces for p in (own, swap(own, "dp", 1))]
    grads = [grad_b, swap(grad_b, "mp", 1), across_b, swap(across_b, "mp", 1)]
    table_grad = table_back(place, grads, q_cut, grad_self, unit, row_dev, near=[pieces[2], pieces[4], pieces[6]])
    across_a = swap(grad_a, "mp", 2)
    grads = [grad_a, swap(grad_a, "mp", 1), across_a, swap(across_a, "mp", 1)]
    table_grad = table_back(place, grads, q_cut, grad_self, 0, row_dev, table_grad, near=[pieces[1]])
    q_grad = widen(exchange(q_pieces, "dp").reshape(-1, columns), after=[table_grad])
    w_grad = collect(place, pieces, after=[table_grad])
    return (
        embedding,
        table_grad,
        q_grad,
        q_bias_grad.reshape(columns),
        w_grad,
        w_bias_grad.reshape(columns),
        penalty.reshape(()),
    )


def solution(mesh):
    placed = (
        P("dp", "mp"),
        P(None, "mp"),
        P("mp"),
        P(None, "mp"),
        P("mp"),
        P("dp", None),
        P("dp"),
        P("dp", None),
        P("dp", "mp"),
    )
    return jax.shard_map(
        shards,
        mesh=mesh,
        in_specs=placed,
        out_specs=(
            P("dp", "mp"),
            P("dp", "mp"),
            P(None, "mp"),
            P("mp"),
            P(None, "mp"),
            P("mp"),
            P(),
        ),
        check_vma=False,
    )
```

```python
import collections
import functools

import jax
import jax.numpy as jnp
from jax import lax
from jax.experimental import pallas as pl
from jax.experimental.pallas import tpu as pltpu
from jax.sharding import PartitionSpec as P

epsilon = 1e-06
penalty_rate = 0.01
bf16, f32, i32, i16 = jnp.bfloat16, jnp.float32, jnp.int32, jnp.int16
bucket_rows = 256
lane_tile = 128
weight_unit = 32767.0
code_step = 64
extra_rows = 16
mib = 1024 * 1024
step_rows = 1024
expected_us = collections.defaultdict(
    lambda: 0.001,
    hidden_slope=5,
    self_half=3,
    combine=1,
    w_back=4,
    rows_back=16,
    add=20,
    add_some=1,
    add_pairs=2,
    table_back=20,
    cut=1,
    collect=2,
    widen=1,
)


def dot(a, b, contract):
    return lax.dot_general(a, b, ((contract[:1], contract[1:]), ((), ())), preferred_element_type=f32)


def gelu_parts(values):
    c = 0.7978845608028654
    squared = values * values
    t = jnp.tanh(c * values * (1.0 + 0.044715 * squared))
    half = 0.5 * (1.0 + t)
    slope = half + 0.5 * values * (1.0 - t * t) * (c * (1.0 + 3 * 0.044715 * squared))
    return values * half, slope


def size(dims, dtype):
    rows = dims[-2] if len(dims) > 1 else 1
    rest = 1
    for d in dims[:-2]:
        rest *= d
    return rest * (-(-rows // 16) * 16) * (-(-dims[-1] // 128) * 128) * jnp.dtype(dtype).itemsize


def far(array):
    return pltpu.with_memory_space_constraint(array, pltpu.HBM)


def far_shape(dims, dtype):
    return pltpu.HBM(dims, dtype)


def call(kernel, name, operands, outs, grid=(1,), scratch=(), after=(), near=(), aliases={}, spare=8):
    after = (*map(far, after), *near)
    specs, arrays, need = [], [], 0
    for operand in operands:
        array, spec = operand if isinstance(operand, tuple) else (operand, whole(operand))
        specs.append(spec)
        arrays.append(array)
        if spec is not smem:
            need += (2 if isinstance(operand, tuple) else 1) * size(spec.block_shape, array.dtype)
    for spec, out in outs:
        need += 2 * size(spec.block_shape, out.dtype)
    for item in scratch:
        need += size(item.shape, item.dtype)
    count = len(arrays)
    inner = lambda *refs: kernel(*refs[:count], *refs[count + len(after) :])
    return pl.pallas_call(
        inner,
        grid=grid,
        in_specs=specs + [pl.BlockSpec(memory_space=pl.ANY)] * len(after),
        out_specs=[o[0] for o in outs],
        out_shape=[o[1] for o in outs],
        scratch_shapes=list(scratch),
        input_output_aliases=dict(aliases),
        compiler_params=pltpu.CompilerParams(vmem_limit_bytes=need + spare * mib),
        cost_estimate=pl.CostEstimate(
            flops=int(expected_us[name] * 1.15e9), bytes_accessed=int(expected_us[name] * 3.69e6), transcendentals=0
        ),
        name=name,
    )(*arrays, *after)


def full(dims, dtype, kind=jax.ShapeDtypeStruct):
    return whole(shape(dims, dtype)), kind(dims, dtype)


def shape(dims, dtype):
    return jax.ShapeDtypeStruct(dims, dtype)


def whole(array):
    return pl.BlockSpec(array.shape, lambda *_: (0,) * array.ndim)


smem = pl.BlockSpec(memory_space=pltpu.SMEM)


def swap(array, axis, bits):
    size = lax.axis_size(axis)
    return lax.ppermute(array, axis, [(i, i ^ bits) for i in range(size)])


def halves(values):
    high = values.astype(bf16)
    return high, (values - high.astype(f32)).astype(bf16)


def exchange(array, axes):
    return lax.all_to_all(array, axes, split_axis=0, concat_axis=0, tiled=True)


def rows_at(ref, start, size):
    return ref.at[pl.ds(pl.multiple_of(start, size), size)]


def row_blocks(block, columns):
    return pl.BlockSpec((block, columns), lambda i: (i, 0))


def each_chunk(step, counts, run):
    first = 0
    for k, count in enumerate(counts):
        pl.when((step >= first) & (step < first + count))(functools.partial(run, k))
        first += count


def chunk_spec(block, columns, first, count):
    return pl.BlockSpec((block, columns), lambda i: (jnp.clip(i - first, 0, count - 1), 0))


def chunk_specs(chunks, block):
    specs, first = [], 0
    for a in chunks:
        count = a.shape[0] // block
        specs.append(chunk_spec(block, a.shape[1], first, count))
        first += count
    return specs


def low_kernel(count, *refs):
    for i in range(count):
        refs[count + i][...] = refs[i][...].astype(bf16)


def low(pieces, steps, after=(), near=()):
    operands, outs = [], []
    for array, first, rows in pieces:
        block, columns = rows // steps, array.shape[1]
        operands.append(
            (far(array), pl.BlockSpec((block, columns), functools.partial(lambda f, i: (f + i, 0), first // block)))
        )
        outs.append((row_blocks(block, columns), far_shape((rows, columns), bf16)))
    return call(functools.partial(low_kernel, len(pieces)), "low", operands, outs, grid=(steps,), after=after, near=near)


def gate_kernel(*refs):
    del refs


def gate(array, after):
    return pl.pallas_call(
        gate_kernel,
        in_specs=[pl.BlockSpec(memory_space=pl.ANY)] * (1 + len(after)),
        out_specs=pl.BlockSpec(memory_space=pl.ANY),
        out_shape=shape(array.shape, array.dtype),
        input_output_aliases={0: 0},
        compiler_params=pltpu.CompilerParams(vmem_limit_bytes=mib),
        cost_estimate=pl.CostEstimate(flops=1, bytes_accessed=1, transcendentals=0),
        name="gate",
    )(array, *after)


def slots_kernel(row_dev, place_ref, ids_ref, counts_ref, importance_ref, out_ref):
    del place_ref
    ids = ids_ref[...]
    index = lax.broadcasted_iota(i32, ids.shape, 0)
    raw = jnp.where(index < counts_ref[...], importance_ref[...], 0.0)
    weight = raw / jnp.sum(raw, axis=0, keepdims=True)
    bucket = jnp.where(weight > 0.0, ids // bucket_rows, -1)
    within = ids - (ids // bucket_rows) * bucket_rows
    merged = jnp.zeros_like(weight)
    rank = jnp.zeros_like(bucket)
    for k in range(ids.shape[0]):
        merged = merged + jnp.where(ids == ids[k : k + 1, :], weight[k : k + 1, :], 0.0)
        rank = rank + jnp.where((bucket == bucket[k : k + 1, :]) & (index > k), 1, 0)
    amount = jnp.round(merged * weight_unit).astype(i32)
    per = row_dev // bucket_rows
    for d in range(out_ref.shape[0]):
        mine = (bucket >= d * per) & (bucket < (d + 1) * per)
        out_ref[d, 0] = jnp.where(mine, (bucket - d * per) * code_step + rank, -1).astype(i16)
        out_ref[d, 1] = within.astype(i16)
        out_ref[d, 2] = amount.astype(i16)


def make_slots(place, neighbours, counts, importance, row_dev, groups, after=()):
    node_dev, slots_node = neighbours.shape
    return call(
        functools.partial(slots_kernel, row_dev),
        "slots",
        [(place, smem), far(neighbours.T), far(counts.reshape(1, node_dev)), far(importance.T)],
        [full((groups, 3, slots_node, node_dev), i16)],
        after=after,
    )[0]


def spread_kernel(slots_ref, out_ref, all_ref, row_ref, amount_ref):
    _, _, slots_node, lanes = slots_ref.shape
    buckets = out_ref.shape[1] // bucket_rows
    tiles = lanes // lane_tile
    codes = slots_ref[0, 0].astype(i32)
    depth = jnp.max(jnp.where(codes >= 0, (codes & (code_step - 1)) + 1, 0).astype(f32)).astype(i32)
    for t in range(tiles):
        at = slice(t * lane_tile, (t + 1) * lane_tile)
        all_ref[t, 0] = codes[:, at].astype(f32)
        all_ref[t, 1] = slots_ref[0, 1, :, at].astype(i32).astype(f32)
        all_ref[t, 2] = slots_ref[0, 2, :, at].astype(i32).astype(f32) * (1.0 / weight_unit)
    eight = lax.broadcasted_iota(i32, (8, lane_tile), 0).astype(f32)

    def extract(t, first):
        target = eight + first
        for start in range(0, buckets, 8):
            some = range(start, min(start + 8, buckets))
            rows = [jnp.full((8, lane_tile), -1.0, f32) for _ in some]
            amounts = [jnp.zeros((8, lane_tile), f32) for _ in some]
            for k in range(slots_node):
                code = jnp.broadcast_to(all_ref[t, 0, k : k + 1, :], (8, lane_tile))
                row = jnp.broadcast_to(all_ref[t, 1, k : k + 1, :], (8, lane_tile))
                amount = jnp.broadcast_to(all_ref[t, 2, k : k + 1, :], (8, lane_tile))
                for i, b in enumerate(some):
                    hit = code == target + float(b * code_step)
                    rows[i] = jnp.where(hit, row, rows[i])
                    amounts[i] = jnp.where(hit, amount, amounts[i])
            for i, b in enumerate(some):
                row_ref[t, b] = rows[i]
                amount_ref[t, b] = amounts[i]

    tall = (bucket_rows // 16, 16, lane_tile)
    row_index = (lax.broadcasted_iota(i32, tall, 0) * 16 + lax.broadcasted_iota(i32, tall, 1)).astype(f32).astype(bf16)

    def place_all(count, add):
        def one(b, carry):
            at = pl.ds(pl.multiple_of(b * bucket_rows, bucket_rows), bucket_rows)
            for t in range(tiles):
                lane = slice(t * lane_tile, (t + 1) * lane_tile)
                total = out_ref[0, at, lane].reshape(tall) if add else jnp.zeros(tall, bf16)
                for j in range(count):
                    row = jnp.broadcast_to(row_ref[t, b, j : j + 1, :], tall[1:]).astype(bf16)
                    amount = jnp.broadcast_to(amount_ref[t, b, j : j + 1, :], tall[1:]).astype(bf16)
                    total = jnp.where(row_index == row[None], amount[None], total)
                out_ref[0, at, lane] = total.reshape(bucket_rows, lane_tile)
            return carry

        lax.fori_loop(0, buckets, one, 0)

    for t in range(tiles):
        extract(t, 0.0)
    for low, high in ((0, 3), (4, 4), (5, 5), (6, 6), (7, slots_node)):

        @pl.when((depth >= low) & (depth <= high))
        def _():
            place_all(min(high, 8), False)

    def more(p, carry):
        for t in range(tiles):
            extract(t, (p * 8).astype(f32))
        place_all(8, True)
        return carry

    lax.fori_loop(1, (depth + 7) // 8, more, 0)


def spread(slots, first, count, row_dev, near=()):
    _, _, slots_node, node_dev = slots.shape
    tiles = node_dev // lane_tile
    buckets = row_dev // bucket_rows
    return call(
        spread_kernel,
        "spread",
        [(slots, pl.BlockSpec((1, 3, slots_node, node_dev), lambda i: (first + i, 0, 0, 0)))],
        [(pl.BlockSpec((1, row_dev, node_dev), lambda i: (i, 0, 0)), shape((count, row_dev, node_dev), bf16))],
        grid=(count,),
        scratch=[
            pltpu.VMEM((tiles, 3, slots_node, lane_tile), f32),
            pltpu.VMEM((tiles, buckets, 8, lane_tile), f32),
            pltpu.VMEM((tiles, buckets, 8, lane_tile), f32),
        ],
        near=near,
    )[0]


def hidden_kernel(sides, want, place_ref, *refs):
    table, q_ref, bias_ref, outs = refs[:sides], refs[sides], refs[sides + 1], refs[sides + 2 :]
    width = table[0].shape[1]
    pre = bias_ref[...]
    for j in range(sides):
        pre = pre + dot(table[j][...], rows_at(q_ref, (place_ref[1] ^ j) * width, width)[...], (1, 0))
    value, slope = gelu_parts(pre)
    if want == "value":
        outs[0][...] = value.astype(bf16).T
    else:
        outs[0][...] = slope.astype(bf16)


def hidden(place, table, q_low, bias, want, after=(), near=()):
    rows, width = table[0].shape
    columns = q_low.shape[1]
    sides = len(table)
    block = min(rows, 512)
    if want == "value":
        out = (pl.BlockSpec((columns, block), lambda i: (0, i)), shape((columns, rows), bf16))
    else:
        out = (row_blocks(block, columns), far_shape((rows, columns), bf16))
    return call(
        functools.partial(hidden_kernel, sides, want),
        "hidden_" + want,
        [(place, smem)]
        + [(a if want == "value" else far(a), row_blocks(block, width)) for a in table]
        + [far(q_low), far(bias.reshape(1, columns))],
        [out],
        grid=(rows // block,),
        after=after,
        near=near,
    )[0]


def pool_kernel(last, parts, counts, *refs):
    hidden_refs, refs = refs[: len(counts)], refs[len(counts) :]
    views = sum(counts)
    matrix, refs = refs[: parts * views], refs[parts * views :]
    groups, rows, nodes = matrix[0].shape
    steps = pl.num_programs(0) // parts

    def one_part(p):
        for g in range(groups):
            total, v = None, p * views
            for hidden_ref, count in zip(hidden_refs, counts):
                for k in range(count):
                    term = dot(hidden_ref[:, k * rows : (k + 1) * rows], matrix[v][g], (1, 0))
                    total, v = term if total is None else total + term, v + 1
            at = slice(g * nodes, (g + 1) * nodes)
            if len(refs) > 1:
                total = total + refs[0][:, at]
            if last:
                refs[-1][at, :] = total.T.astype(bf16)
            else:
                refs[-1][:, at] = total

    each_chunk(pl.program_id(0), [steps] * parts, one_part)


def pool(hidden_t, matrix, first, so_far, step_rows, last, near=()):
    columns = hidden_t[0].shape[0]
    per, _, node_dev = matrix[0].shape
    parts, counts = len(matrix), [a.shape[1] // step_rows for a in hidden_t]
    nodes = parts * per * node_dev
    steps = per // 2
    total_block = pl.BlockSpec((columns, 2 * node_dev), lambda i: (0, i))
    operands = list(hidden_t)
    for p in range(parts):
        for v in range(sum(counts)):
            index = functools.partial(lambda p, v, i: (jnp.clip(i - p * steps, 0, steps - 1), v, 0), p, first // step_rows + v)
            operands.append((matrix[p], pl.BlockSpec((2, step_rows, node_dev), index)))
    return call(
        functools.partial(pool_kernel, last, parts, counts),
        "pool",
        operands + ([] if so_far is None else [(so_far, total_block)]),
        [
            (row_blocks(2 * node_dev, columns), shape((nodes, columns), bf16))
            if last
            else (total_block, shape((columns, nodes), f32))
        ],
        grid=(parts * steps,),
        near=near,
    )[0]


def first_rows(table, nodes):
    return [(far(a), pl.BlockSpec((nodes, a.shape[1]), lambda *_: (0, 0))) for a in table]


def self_kernel(sides, place_ref, *refs):
    own, (w_ref, bias_ref, cotangent_ref), outs = refs[:sides], refs[sides : sides + 3], refs[sides + 3 : -1]
    pre_ref = refs[-1]
    width = own[0].shape[1]
    pre = bias_ref[...]
    for j in range(sides):
        pre = pre + dot(own[j][...], rows_at(w_ref, (place_ref[1] ^ j) * width, width)[...], (1, 0))
    pre_ref[...] = pre
    few, columns = outs[0].shape[0], pre.shape[1]
    for j in range(sides):
        at = (place_ref[1] ^ j) * few
        outs[j][:, 0:columns] = rows_at(pre_ref, at, few)[...]
        outs[j][:, columns:] = rows_at(cotangent_ref, at, few)[...]


def self_half(place, table, w_self, bias, cotangent, near=()):
    nodes, columns = cotangent.shape
    sides = len(table)
    return call(
        functools.partial(self_kernel, sides),
        "self_half",
        [(place, smem)] + first_rows(table, nodes) + [far(w_self), far(bias.reshape(1, columns)), far(cotangent)],
        [full((nodes // sides, 2 * columns), f32, far_shape)] * sides,
        scratch=[pltpu.VMEM((nodes, columns), f32)],
        near=near,
    )


def combine_kernel(node_total, sides, parts_ref, *refs):
    early, w_refs = refs[:sides], refs[sides : 2 * sides]
    grad_ref, pooled_ref, late = refs[2 * sides], refs[2 * sides + 1], refs[2 * sides + 2 :]
    groups, _, few, columns = parts_ref.shape
    pooled = []
    for m in range(sides):
        total = parts_ref[0, m].astype(f32)
        for g in range(1, groups):
            total = total + parts_ref[g, m].astype(f32)
        pooled.append(total.astype(bf16))
    pooled = jnp.concatenate(pooled, axis=1)
    pooled_ref[...] = pooled
    activated, slope, squares, cross = [], [], 0.0, 0.0
    for j in range(sides):
        pre = early[j][:, 0:columns] + dot(pooled, w_refs[j][...], (1, 0))
        a, s = gelu_parts(pre)
        activated.append(a)
        slope.append(s)
        squares = squares + jnp.sum(a * a, axis=1, keepdims=True)
        cross = cross + jnp.sum(a * early[j][:, columns:], axis=1, keepdims=True)
    scale = lax.rsqrt(squares + epsilon)
    pull = cross * scale * scale * scale
    grad_pooled = 0.0
    square_high, square_low = halves(jnp.sum(squares, axis=0, keepdims=True))
    index = lax.broadcasted_iota(i32, (extra_rows, late[0].shape[1]), 0)
    extra = jnp.where(
        index == 0, square_high.astype(f32), jnp.where(index == 1, square_low.astype(f32), 0.0)
    ).astype(bf16)
    for j in range(sides):
        grad_act = early[j][:, columns:] * scale - activated[j] * pull + (2.0 * penalty_rate / node_total) * activated[j]
        grad = (grad_act * slope[j]).astype(bf16)
        grad_pooled = grad_pooled + dot(grad, w_refs[j][...], (1, 1))
        late[j][0:few, 0:columns] = (activated[j] * scale).astype(bf16)
        late[j][0:few, columns:] = grad
        late[j][few:, :] = extra
    for m in range(sides):
        part = grad_pooled[:, m * columns : (m + 1) * columns].astype(bf16)
        for g in range(groups):
            grad_ref[g, m] = part


def combine(node_total, parts, early, w_pooled, after=()):
    groups, sides, few, columns = parts.shape
    return call(
        functools.partial(combine_kernel, node_total, sides),
        "combine",
        [parts, *map(far, early), *map(far, w_pooled)],
        [full(parts.shape, bf16), full((few, sides * columns), bf16, far_shape)]
        + [full((few + extra_rows, 2 * columns), bf16, far_shape)] * sides,
        after=after,
    )


def w_back_kernel(sides, place_ref, *refs):
    own, late, pooled = refs[:sides], refs[sides : 2 * sides], refs[2 * sides : 3 * sides]
    (w_ref, emb_ref, even_ref, odd_ref, extra_ref, *self_refs), scratch = refs[3 * sides : -3], refs[-3:]
    grad_ref, pooled_ref, total_ref = scratch
    nodes, columns = emb_ref.shape
    few = nodes // sides
    squares = 0.0
    for j in range(sides):
        at = (place_ref[1] ^ j) * few
        rows_at(emb_ref, at, few)[...] = late[j][0:few, 0:columns].astype(f32)
        rows_at(grad_ref, at, few)[...] = late[j][0:few, columns:]
        rows_at(pooled_ref, at, few)[...] = pooled[j][...]
        squares = squares + late[j][few : few + 1, 0:columns].astype(f32)
        squares = squares + late[j][few + 1 : few + 2, 0:columns].astype(f32)
    grad = grad_ref[...]
    for j in range(sides):
        side = place_ref[1] ^ j
        rows_at(total_ref, side * columns, columns)[...] = dot(own[j][...], grad, (0, 0))
        self_refs[j][...] = dot(grad, rows_at(w_ref, side * columns, columns)[...], (1, 1)).astype(bf16)
    total_ref[sides * columns :, :] = dot(pooled_ref[...], grad, (0, 0))
    bias_high, bias_low = halves(jnp.sum(grad.astype(f32), axis=0, keepdims=True))
    square_high, square_low = halves(squares)
    index = lax.broadcasted_iota(i32, (extra_rows, columns), 0)
    extra = jnp.zeros(index.shape, f32)
    for i, row in enumerate((bias_high, bias_low, square_high, square_low)):
        extra = jnp.where(index == 2 + i, row.astype(f32), extra)
    extra_ref[...] = extra.astype(bf16)
    count, piece, _ = even_ref.shape
    for s in range(count):
        even_ref[s] = rows_at(total_ref, (place_ref[0] ^ (2 * s)) * piece, piece)[...].astype(bf16)
        odd_ref[s] = rows_at(total_ref, (place_ref[0] ^ (2 * s + 1)) * piece, piece)[...].astype(bf16)


def w_back(place, table, late, pooled, w_self, node_dev, groups, after=()):
    sides = len(table)
    rows, columns = 2 * w_self.shape[0], w_self.shape[1]
    half = full((groups // 2, rows // groups, columns), bf16, far_shape)
    return call(
        functools.partial(w_back_kernel, sides),
        "w_back",
        [(place, smem)] + first_rows(table, node_dev) + [*late, *pooled, far(w_self)],
        [full((node_dev, columns), f32, far_shape), half, half]
        + [full((extra_rows, columns), bf16, far_shape)]
        + [full((node_dev, columns), bf16, far_shape)] * sides,
        scratch=[
            pltpu.VMEM((node_dev, columns), bf16),
            pltpu.VMEM((node_dev, sides * columns), bf16),
            pltpu.VMEM((rows, columns), f32),
        ],
        after=after,
    )


def add_pairs_kernel(own_ref, other_ref, *outs):
    for i, out in enumerate(outs):
        out[...] = (own_ref[i].astype(f32) + other_ref[i].astype(f32)).astype(bf16)


def add_pairs(own, other, after=(), near=()):
    count, rows, columns = own.shape
    return call(
        add_pairs_kernel, "add_pairs", [far(own), other], [full((rows, columns), bf16)] * count, after=after, near=near
    )


def add_some_kernel(count, *refs):
    total = refs[0][...].astype(f32)
    for ref in refs[1:count]:
        total = total + ref[...].astype(f32)
    refs[count][...] = total.astype(bf16)


def add_some(parts, after=()):
    return call(
        functools.partial(add_some_kernel, len(parts)), "add_some", parts, [full(parts[0].shape, bf16)], after=after
    )[0]


def collect_kernel(count, place_ref, *refs):
    piece = refs[0].shape[0]
    for i in range(count):
        rows_at(refs[count], (place_ref[0] ^ i) * piece, piece)[...] = refs[i][...].astype(f32)


def collect(place, pieces, after=()):
    rows, columns = pieces[0].shape
    return call(
        functools.partial(collect_kernel, len(pieces)),
        "collect",
        [(place, smem), *pieces],
        [full((len(pieces) * rows, columns), f32, far_shape)],
        after=after,
    )[0]


def add_kernel(scale, parts_ref, piece_ref, q_bias_ref, w_bias_ref, scalar_ref):
    groups, rows, _ = parts_ref.shape
    total = parts_ref[0].astype(f32)
    for g in range(1, groups):
        total = total + parts_ref[g].astype(f32)
    piece = rows - extra_rows
    low = total[0:piece, :].astype(bf16)
    for g in range(groups):
        piece_ref[g] = low
    pairs = [total[piece + 2 * i : piece + 2 * i + 1, :] + total[piece + 2 * i + 1 : piece + 2 * i + 2, :] for i in range(3)]
    q_bias_ref[...] = pairs[0]
    w_bias_ref[...] = pairs[1]
    scalar_ref[...] = scale * pairs[2][:, 0:1]


def add(parts, scale, after=()):
    groups, rows, columns = parts.shape
    return call(
        functools.partial(add_kernel, scale),
        "add",
        [parts],
        [full((groups, rows - extra_rows, columns), bf16), full((1, columns), f32), full((1, columns), f32), full((1, 1), f32)],
        after=after,
    )


def widen_kernel(low_ref, out_ref):
    out_ref[...] = low_ref[...].astype(f32)


def widen(low, after=()):
    rows, columns = low.shape
    block = rows // 2
    return call(
        widen_kernel,
        "widen",
        [(low, row_blocks(block, columns))],
        [(row_blocks(block, columns), far_shape((rows, columns), f32))],
        grid=(2,),
        after=after,
    )[0]


def rows_back_kernel(chunk_counts, grad_counts, sides, parts, place_ref, *refs):
    chunks = len(chunk_counts)
    matrix, refs = refs[:parts], refs[parts:]
    pooled_ref, slopes, table = refs[0], refs[1 : 1 + chunks], refs[1 + chunks : 1 + chunks + chunks * sides]
    extra_ref, rest = refs[1 + chunks + chunks * sides], refs[2 + chunks + chunks * sides :]
    grad_refs, (q_ref, total_ref, bias_ref, low_ref) = rest[: len(grad_counts)], rest[len(grad_counts) :]
    step = pl.program_id(0)
    matrix = jnp.concatenate([part[g] for part in matrix for g in range(part.shape[0])], axis=1)
    summed = dot(matrix, pooled_ref[...], (1, 0))
    width = table[0].shape[1]

    @pl.when(step == 0)
    def _():
        bias_ref[...] = jnp.zeros_like(bias_ref)
        total_ref[...] = jnp.zeros_like(total_ref)

    def in_chunk(k):
        grad = summed * slopes[k][...].astype(f32)
        bias_ref[...] += jnp.sum(grad, axis=0, keepdims=True)
        grad = grad.astype(bf16)
        low_ref[...] = grad
        for j in range(sides):
            total_ref[j] += dot(grad, table[k * sides + j][...], (0, 0))

    def put(k):
        grad_refs[k][...] = low_ref[...]

    each_chunk(step, chunk_counts, in_chunk)
    each_chunk(step, grad_counts, put)

    @pl.when(step == pl.num_programs(0) - 1)
    def _():
        high, low = halves(bias_ref[...])
        groups, rows, columns = q_ref.shape
        index = lax.broadcasted_iota(i32, (extra_rows, columns), 0)
        extra = extra_ref[...].astype(f32)
        extra = jnp.where(index == 0, high.astype(f32), jnp.where(index == 1, low.astype(f32), extra)).astype(bf16)
        piece = rows - extra_rows
        per = width // piece
        for g in range(groups):
            q_ref[g, piece:, :] = extra
        for j in range(sides):
            flat = total_ref[j].T.astype(bf16)
            for part in range(per):
                q_ref[(place_ref[1] ^ j) * per + part, 0:piece, :] = flat[part * piece : (part + 1) * piece, :]


def rows_back(place, matrix, pooled, slopes, table, extra, grad_rows, near=()):
    sides = len(table[0])
    per, row_dev, node_dev = matrix[0].shape
    groups = per * len(matrix)
    columns, width = pooled.shape[1], table[0][0].shape[1]
    block = min(min(a.shape[0] for a in slopes), step_rows * 2048 // (groups * node_dev))
    by_side = [chunk_specs([part[j] for part in table], block) for j in range(sides)]
    grads = [shape((rows, columns), bf16) for rows in grad_rows]
    return call(
        functools.partial(rows_back_kernel, [a.shape[0] // block for a in slopes], [r // block for r in grad_rows], sides, len(matrix)),
        "rows_back",
        [(place, smem)]
        + [(far(part), pl.BlockSpec((per, block, node_dev), lambda i: (0, i, 0))) for part in matrix]
        + [pooled]
        + list(zip(map(far, slopes), chunk_specs(slopes, block)))
        + [(far(table[k][j]), by_side[j][k]) for k in range(len(table)) for j in range(sides)]
        + [far(extra)],
        [(spec, far_shape(a.shape, bf16)) for spec, a in zip(chunk_specs(grads, block), grads)]
        + [full((groups, sides * width // groups + extra_rows, columns), bf16)],
        grid=(row_dev // block,),
        scratch=[
            pltpu.VMEM((sides, columns, width), f32),
            pltpu.VMEM((1, columns), f32),
            pltpu.VMEM((block, columns), bf16),
        ],
        near=near,
    )


def table_back_kernel(sides, nodes, with_self, place_ref, *refs):
    grads, qs, self_refs, out_ref = refs[:sides], refs[sides : 2 * sides], refs[2 * sides : -1], refs[-1]
    width = out_ref.shape[1]
    total = dot(grads[0][...], qs[0][...], (1, 1))
    for j in range(1, sides):
        total = total + dot(grads[j][...], qs[j][...], (1, 1))
    out_ref[...] = total
    if not with_self:
        return

    @pl.when(pl.program_id(0) == 0)
    def _():
        own = self_refs[0][...].astype(f32)
        for ref in self_refs[1:sides]:
            own = own + ref[...].astype(f32)
        out_ref[0:nodes, :] += own


def table_back(place, grads, qs, grad_self, first, row_dev, so_far=None, near=()):
    sides = len(grads)
    rows, columns = grads[0].shape
    nodes, width = grad_self[0].shape
    block = min(rows, 512)
    operands = [(place, smem)] + [(far(a), row_blocks(block, columns)) for a in grads] + [*map(far, qs), *map(far, grad_self)]
    return call(
        functools.partial(table_back_kernel, sides, nodes, first == 0),
        "table_back",
        operands,
        [(pl.BlockSpec((block, width), lambda i: (first // block + i, 0)), far_shape((row_dev, width), f32))],
        grid=(rows // block,),
        after=() if so_far is None else [so_far],
        near=near,
        aliases={} if so_far is None else {len(operands): 0},
    )[0]


def cut_kernel(sides, place_ref, q_ref, *outs):
    width = outs[0].shape[0]
    for j in range(sides):
        outs[j][...] = rows_at(q_ref, (place_ref[1] ^ j) * width, width)[...]


def cut_rows(place, q_low, sides, after=()):
    rows, columns = q_low.shape
    return call(
        functools.partial(cut_kernel, sides),
        "cut",
        [(place, smem), far(q_low)],
        [full((rows // sides, columns), bf16, far_shape)] * sides,
        after=after,
    )


def all_sides(array):
    across = swap(array, "mp", 2)
    return [array, swap(array, "mp", 1), across, swap(across, "mp", 1)]


def shards(table, q_weight, q_bias, w_weight, w_bias, neighbours, counts, importance, cotangent):
    groups = lax.axis_size("dp")
    sides = lax.axis_size("mp")
    row_dev, width = table.shape
    node_dev, _ = neighbours.shape
    node_total = node_dev * groups
    columns = q_weight.shape[1]
    few = node_dev // sides
    place = jnp.stack([lax.axis_index("dp"), lax.axis_index("mp")]).astype(i32)

    unit = row_dev // 4
    (low_a,) = low([(table, 0, unit)], 1)
    low_b, low_c = low([(table, unit, 2 * unit), (table, 3 * unit, unit)], 2, after=[low_a])
    across_a, beside_a = swap(low_a, "mp", 2), swap(low_a, "mp", 1)
    slots = make_slots(place, neighbours, counts, importance, row_dev, groups, after=[low_b])
    half = sides * width
    q_low, w_self, w_pooled = low([(q_weight, 0, half), (w_weight, 0, half), (w_weight, half, half)], 4, near=[slots])
    low_b = gate(low_b, [across_a])
    across_b, beside_b = swap(low_b, "mp", 2), swap(low_b, "mp", 1)
    slots = exchange(slots, "dp")

    part_a = [low_a, beside_a, across_a, swap(across_a, "mp", 1)]
    hidden_a = hidden(place, part_a, q_low, q_bias, "value")
    first = spread(slots, 0, groups // 2, row_dev, near=[hidden_a])
    across_b = gate(across_b, [first])
    low_c = gate(low_c, [across_b])
    across_c, beside_c = swap(low_c, "mp", 2), swap(low_c, "mp", 1)
    matrix = [first, spread(slots, groups // 2, groups // 2, row_dev)]
    part_b = [low_b, beside_b, across_b, swap(across_b, "mp", 1)]
    hidden_b = hidden(place, part_b, q_low, q_bias, "value", near=[matrix[1]])
    so_far = pool([hidden_a, hidden_b], matrix, 0, None, unit, False)
    across_c = gate(across_c, [hidden_b])
    part_c = [low_c, beside_c, across_c, swap(across_c, "mp", 1)]
    parts = [part_a, part_b, part_c]
    hidden_c = hidden(place, part_c, q_low, q_bias, "value", near=[so_far])
    w_pooled = all_sides(gate(w_pooled, [matrix[1]]))
    part_sums = pool([hidden_c], matrix, 3 * unit, so_far, unit, True)
    pooled = exchange(part_sums.reshape(groups * sides, few, columns), ("dp", "mp"))

    early = self_half(place, part_a, w_self, w_bias, cotangent, near=[part_sums, w_pooled[2]])
    early = [early[0]] + [swap(early[j], "mp", j) for j in range(1, sides)]
    slope = [hidden(place, part, q_low, q_bias, "slope", after=[early[0]]) for part in parts]

    grad_pooled, pooled, *late = combine(
        node_total, pooled.reshape(groups, sides, few, columns), early, w_pooled, after=slope
    )
    grad_pooled = exchange(grad_pooled.reshape(groups * sides, few, columns), ("dp", "mp")).reshape(node_total, columns)
    late = [late[0]] + [swap(late[j], "mp", j) for j in range(1, sides)]
    embedding, even, odd, extra, *grad_self = w_back(
        place, part_a, late, all_sides(pooled), w_self, node_dev, groups
    )
    q_cut = cut_rows(place, q_low, sides, after=[slope[0]])
    q_cut = [q_cut[0]] + [swap(q_cut[j], "mp", j) for j in range(1, sides)]
    grad_self = [grad_self[0]] + [swap(grad_self[j], "mp", j) for j in range(1, sides)]

    grad_a, grad_b, q_parts = rows_back(place, matrix, grad_pooled, slope, parts, extra, [unit, 3 * unit], near=[q_cut[2]])
    pairs = add_pairs(even, swap(odd, "dp", 1), after=[grad_a], near=[grad_self[1], grad_self[2], grad_self[3]])
    count = groups // 2
    pairs = [pairs[0]] + [swap(pairs[s], "dp", 2 * s) for s in range(1, count)]
    grad_b = gate(grad_b, [pairs[0]])
    across_b = swap(grad_b, "mp", 2)
    piece = add_some(pairs)
    pieces = [piece] + [swap(piece, "dp", 2 * s) for s in range(1, count)]
    q_pieces, q_bias_grad, w_bias_grad, penalty = add(
        exchange(q_parts, "dp"), penalty_rate / node_total, after=[piece]
    )
    pieces = [p for own in pieces for p in (own, swap(own, "dp", 1))]
    grads = [grad_b, swap(grad_b, "mp", 1), across_b, swap(across_b, "mp", 1)]
    table_grad = table_back(place, grads, q_cut, grad_self, unit, row_dev, near=[pieces[2], pieces[4], pieces[6]])
    across_a = swap(grad_a, "mp", 2)
    grads = [grad_a, swap(grad_a, "mp", 1), across_a, swap(across_a, "mp", 1)]
    table_grad = table_back(place, grads, q_cut, grad_self, 0, row_dev, table_grad, near=[pieces[1]])
    q_grad = widen(exchange(q_pieces, "dp").reshape(-1, columns), after=[table_grad])
    w_grad = collect(place, pieces, after=[table_grad])
    return (
        embedding,
        table_grad,
        q_grad,
        q_bias_grad.reshape(columns),
        w_grad,
        w_bias_grad.reshape(columns),
        penalty.reshape(()),
    )


def solution(mesh):
    placed = (
        P("dp", "mp"),
        P(None, "mp"),
        P("mp"),
        P(None, "mp"),
        P("mp"),
        P("dp", None),
        P("dp"),
        P("dp", None),
        P("dp", "mp"),
    )
    return jax.shard_map(
        shards,
        mesh=mesh,
        in_specs=placed,
        out_specs=(
            P("dp", "mp"),
            P("dp", "mp"),
            P(None, "mp"),
            P("mp"),
            P(None, "mp"),
            P("mp"),
            P(),
        ),
        check_vma=False,
    )
```
